128 devices in a mesh: seq: 64 (over z, y_hi, x, core), tp: 2 (over y_lo).
Axes of the slice: x: 4, y: 4 (y_hi: 2, y_lo: 2; y = y_hi * 2 + y_lo), z: 4, core: 2. Of those that a mesh axis runs over, the one named last changes fastest.
Arguments:
- tokens: bfloat16 [16384, 1024], P('seq'), may hold values from -6 to 6
- cotangent: bfloat16 [16384, 1024], P('seq'), may hold values from -12 to 12
- doc_ids: int32 [64], replicated, may hold values from 0 to 1, as said below
- inward_weight: float32 [1024, 3, 1024], P('seq', None, 'tp'), may hold values from -0.1875 to 0.1875
- inward_first: float32 [1024, 3, 1024], P('seq', None, 'tp'), may hold values from -192 to 192
- inward_second: float32 [1024, 3, 1024], P('seq', None, 'tp'), may hold values from 4096 to 16384
- outward_weight: float32 [1024, 1024], P('seq', 'tp'), may hold values from -0.1875 to 0.1875
- outward_first: float32 [1024, 1024], P('seq', 'tp'), may hold values from -192 to 192
- outward_second: float32 [1024, 1024], P('seq', 'tp'), may hold values from 4096 to 16384
- expand_weight: float32 [1024, 2, 4608], P('seq', None, 'tp'), may hold values from -0.1875 to 0.1875
- expand_first: float32 [1024, 2, 4608], P('seq', None, 'tp'), may hold values from -42.24 to 42.24
- expand_second: float32 [1024, 2, 4608], P('seq', None, 'tp'), may hold values from 212.992 to 868.352
- reduce_weight: float32 [1024, 4608], P('seq', 'tp'), may hold values from -0.09375 to 0.09375
- reduce_first: float32 [1024, 4608], P('seq', 'tp'), may hold values from -102.4 to 102.4
- reduce_second: float32 [1024, 4608], P('seq', 'tp'), may hold values from 1245.184 to 4915.2
- norm_gains: float32 [2, 1024], replicated, may hold values from 0.5 to 1.5
- gains_first: float32 [2, 1024], replicated, may hold values from -204.8 to 204.8
- gains_second: float32 [2, 1024], replicated, may hold values from 4915.2 to 19660.8
- conv_taps: float32 [3, 1024], P(None, 'tp'), may hold values from -2 to 2
- taps_first: float32 [3, 1024], P(None, 'tp'), may hold values from -217.6 to 217.6
- taps_second: float32 [3, 1024], P(None, 'tp'), may hold values from 5406.72 to 21299.2
Outputs:
- block_out: bfloat16 [16384, 1024], P('seq')
- grad_tokens: float32 [16384, 1024], P('seq')
- inward_new: float32 [1024, 3, 1024], P('seq', None, 'tp')
- inward_moment: float32 [1024, 3, 1024], P('seq', None, 'tp')
- inward_square: float32 [1024, 3, 1024], P('seq', None, 'tp')
- outward_new: float32 [1024, 1024], P('seq', 'tp')
- outward_moment: float32 [1024, 1024], P('seq', 'tp')
- outward_square: float32 [1024, 1024], P('seq', 'tp')
- expand_new: float32 [1024, 2, 4608], P('seq', None, 'tp')
- expand_moment: float32 [1024, 2, 4608], P('seq', None, 'tp')
- expand_square: float32 [1024, 2, 4608], P('seq', None, 'tp')
- reduce_new: float32 [1024, 4608], P('seq', 'tp')
- reduce_moment: float32 [1024, 4608], P('seq', 'tp')
- reduce_square: float32 [1024, 4608], P('seq', 'tp')
- gains_new: float32 [2, 1024], replicated
- gains_moment: float32 [2, 1024], replicated
- gains_square: float32 [2, 1024], replicated
- taps_new: float32 [3, 1024], P(None, 'tp')
- taps_moment: float32 [3, 1024], P(None, 'tp')
- taps_square: float32 [3, 1024], P(None, 'tp')
The draws below stay inside these ranges and needn't reach their ends.
Inputs may be any that keep to these rules, and one draw needn't show every extreme that they name: `doc_ids`: non-decreasing over the 64 blocks; both 0 and 1 occur, each on 16 blocks or more.
All inputs are finite; a program needn't handle non-finite values.
Results may differ from the reference program's by a relative error of at most 0.02.
Values may be sent and summed in bfloat16 or wider, within the bound.
No kernel may reach another device: no remote copies, remote signals or barrier semaphores. Data moves between devices by JAX's collectives and lax.ppermute only.
A program may use at most 192 MiB of HBM per device.

```python
import math
import jax
import jax.numpy as jnp
from jax import lax

D = 1024
FF = 4608
TAPS = 3
STEP = 8
TOK_DEV = 256
BLOCKS = 64
TOKENS = 16384


def draw_cotangent(key, part):
    key = jax.random.fold_in(key, 11)
    ramp = jnp.arange(TOKENS, dtype=jnp.float32) / (TOKENS - 1)
    base = jnp.clip(jax.random.normal(key, (TOKENS, D), jnp.float32), -4.0, 4.0)
    row_scale = 1.0 + 2.0 * ramp
    return (base * row_scale[:, None]).astype(jnp.bfloat16)


def draw_doc_ids(key, part):
    key = jax.random.fold_in(key, 23)
    boundary = jax.random.randint(key, (), BLOCKS // 4, 3 * BLOCKS // 4 + 1)
    return (jnp.arange(BLOCKS, dtype=jnp.int32) >= boundary).astype(jnp.int32)


def block_scale(key, dims, split, low, high):
    def one(axis_at, shards_of):
        heights = jax.random.uniform(jax.random.fold_in(jax.random.fold_in(key, 6), axis_at), (shards_of,), jnp.float32, low / len(split), high / len(split))
        return jnp.repeat(jnp.exp(heights), dims[axis_at] // shards_of).reshape((-1,) + (1,) * (len(dims) - axis_at - 1))

    loudness = one(*split[0])
    for cut in split[1:]:
        loudness = loudness * one(*cut)
    return loudness


def scatter_about(key, dims, deviation, reach, pieces=(), kind=jnp.bfloat16):
    gain = block_scale(key, dims, pieces, -0.22, 0.18) if pieces else 1.0
    entries = jax.random.normal(key, dims, jnp.float32) * deviation * gain
    return jnp.minimum(jnp.maximum(entries, -reach), reach).astype(kind)


def setup_inputs(seed: int = 0) -> dict:
    seeds = jax.random.split(jax.random.key(seed), 22)
    tokens = scatter_about(seeds[0], (TOKENS, D), 1.0, 6.0, ((0, 64),))
    cotangent = draw_cotangent(jax.random.fold_in(seeds[21], 71), 0)
    doc_ids = draw_doc_ids(jax.random.fold_in(seeds[21], 71), 0)
    inward_weight = scatter_about(seeds[3], (D, 3, D), D ** -0.5, 0.1875, ((0, 64), (2, 2)), jnp.float32)
    inward_first = scatter_about(seeds[4], (D, 3, D), (0.25 * TOKENS ** 0.5), 192.0, ((0, 64), (2, 2)), jnp.float32)
    inward_second = jnp.clip(jnp.exp(math.log(16384.0) - 1.3862944 * jax.random.uniform(seeds[5], (D, 3, D), jnp.float32) ** block_scale(seeds[5], (D, 3, D), ((0, 64), (2, 2)), -0.2, 0.2)), 4096.0, 16384.0)
    outward_weight = scatter_about(seeds[6], (D, D), D ** -0.5, 0.1875, ((0, 64), (1, 2)), jnp.float32)
    outward_first = scatter_about(seeds[7], (D, D), (0.25 * TOKENS ** 0.5), 192.0, ((0, 64), (1, 2)), jnp.float32)
    outward_second = jnp.clip(jnp.exp(math.log(16384.0) - 1.3862944 * jax.random.uniform(seeds[8], (D, D), jnp.float32) ** block_scale(seeds[8], (D, D), ((0, 64), (1, 2)), -0.2, 0.2)), 4096.0, 16384.0)
    expand_weight = scatter_about(seeds[9], (D, 2, FF), D ** -0.5, 0.1875, ((0, 64), (2, 2)), jnp.float32)
    expand_first = scatter_about(seeds[10], (D, 2, FF), (0.055 * TOKENS ** 0.5), 42.24, ((0, 64), (2, 2)), jnp.float32)
    expand_second = jnp.clip(jnp.exp(math.log(868.352) - 1.40534252 * jax.random.uniform(seeds[11], (D, 2, FF), jnp.float32) ** block_scale(seeds[11], (D, 2, FF), ((0, 64), (2, 2)), -0.2, 0.2)), 212.992, 868.352)
    reduce_weight = scatter_about(seeds[12], (D, FF), FF ** -0.5, 0.09375, ((0, 64), (1, 2)), jnp.float32)
    reduce_first = scatter_about(seeds[13], (D, FF), (0.13 * TOKENS ** 0.5), 102.4, ((0, 64), (1, 2)), jnp.float32)
    reduce_second = jnp.clip(jnp.exp(math.log(4915.2) - 1.3730492 * jax.random.uniform(seeds[14], (D, FF), jnp.float32) ** block_scale(seeds[14], (D, FF), ((0, 64), (1, 2)), -0.2, 0.2)), 1245.184, 4915.2)
    norm_gains = jnp.clip(1.0 + 0.1 * jax.random.normal(seeds[15], (2, D), jnp.float32), 0.5, 1.5)
    gains_first = scatter_about(seeds[16], (2, D), (0.27 * TOKENS ** 0.5), 204.8, (), jnp.float32)
    gains_second = jnp.clip(jnp.exp(jax.random.uniform(seeds[17], (2, D), jnp.float32, math.log(4915.2), math.log(19660.8))), 4915.2, 19660.8)
    conv_taps = scatter_about(seeds[18], (TAPS, D), 0.5, 2.0, ((1, 2),), jnp.float32)
    taps_first = scatter_about(seeds[19], (TAPS, D), (0.28 * TOKENS ** 0.5), 217.6, ((1, 2),), jnp.float32)
    taps_second = jnp.clip(jnp.exp(math.log(21299.2) - 1.3710268 * jax.random.uniform(seeds[20], (TAPS, D), jnp.float32) ** block_scale(seeds[20], (TAPS, D), ((1, 2),), -0.2, 0.2)), 5406.72, 21299.2)
    return {"tokens": tokens, "cotangent": cotangent, "doc_ids": doc_ids, "inward_weight": inward_weight, "inward_first": inward_first, "inward_second": inward_second, "outward_weight": outward_weight, "outward_first": outward_first, "outward_second": outward_second, "expand_weight": expand_weight, "expand_first": expand_first, "expand_second": expand_second, "reduce_weight": reduce_weight, "reduce_first": reduce_first, "reduce_second": reduce_second, "norm_gains": norm_gains, "gains_first": gains_first, "gains_second": gains_second, "conv_taps": conv_taps, "taps_first": taps_first, "taps_second": taps_second}


@jax.custom_vjp
def low(v):
    return lax.optimization_barrier(v.astype(jnp.bfloat16)).astype(jnp.float32)

@jax.custom_vjp
def low_back(v):
    return v

def low_keep(v):
    return (low(v), None)

def low_pass(kept, grad):
    return (grad,)

def back_keep(v):
    return (v, None)

def back_low(kept, grad):
    return (low(grad),)
low.defvjp(low_keep, low_pass)
low_back.defvjp(back_keep, back_low)

def forward(xf, gains, taps, w_in, w_out, w_up, w_down, same_one, same_two):
    best = lax.Precision.HIGHEST
    scale_one = lax.rsqrt(lax.optimization_barrier(jnp.mean(xf * xf, axis=1, keepdims=True)) + 1e-05)
    normed = low(xf * scale_one * gains[0])
    projected = low_back(jnp.einsum('td,dkc->tkc', normed, low(w_in), precision=best))
    gated_in = low(projected[:, 0] * projected[:, 2])
    zero_row = jnp.zeros((1, gated_in.shape[1]), jnp.float32)
    back_one = jnp.concatenate([zero_row, gated_in[:-1]], 0) * same_one
    back_two = jnp.concatenate([zero_row, zero_row, gated_in[:-2]], 0) * same_two
    mixed = taps[2] * gated_in + taps[1] * back_one + taps[0] * back_two
    gated_out = low(projected[:, 1] * mixed)
    mixer = low_back(jnp.einsum('tc,ec->te', gated_out, low(w_out), precision=best))
    resid = xf + mixer
    scale_two = lax.rsqrt(lax.optimization_barrier(jnp.mean(resid * resid, axis=1, keepdims=True)) + 1e-05)
    normed_two = low(resid * scale_two * gains[1])
    gate_up = low_back(jnp.einsum('td,dkf->tkf', normed_two, low(w_up), precision=best))
    act = low(jax.nn.silu(gate_up[:, 0]) * gate_up[:, 1])
    return resid + jnp.einsum('tf,ef->te', act, low(w_down), precision=best)

def adamw(weight, grad, first, second, rate, decay):
    first_new = 0.9 * first + 0.1 * grad
    second_new = 0.95 * second + 0.05 * grad * grad
    step_size = first_new / (1.0 - 0.9 ** STEP) / (jnp.sqrt(second_new / (1.0 - 0.95 ** STEP)) + 1e-08)
    return (weight - rate * (step_size + decay * weight), first_new, second_new)

def reference(tokens, cotangent, doc_ids, inward_weight, inward_first, inward_second, outward_weight, outward_first, outward_second, expand_weight, expand_first, expand_second, reduce_weight, reduce_first, reduce_second, norm_gains, gains_first, gains_second, conv_taps, taps_first, taps_second):
    token_doc = jnp.repeat(doc_ids, TOK_DEV)
    same_one = jnp.concatenate([jnp.zeros((1,), jnp.float32), (token_doc[1:] == token_doc[:-1]).astype(jnp.float32)])[:, None]
    same_two = jnp.concatenate([jnp.zeros((2,), jnp.float32), (token_doc[2:] == token_doc[:-2]).astype(jnp.float32)])[:, None]
    xf = tokens.astype(jnp.float32)

    def wrapped(xv, gains, taps, w_in, w_out, w_up, w_down):
        return forward(xv, gains, taps, w_in, w_out, w_up, w_down, same_one, same_two)
    output, pullback = jax.vjp(wrapped, xf, norm_gains, conv_taps, inward_weight, outward_weight, expand_weight, reduce_weight)
    grads = pullback(cotangent.astype(jnp.float32))
    grad_tokens, grad_gains, grad_taps, grad_in, grad_out, grad_up, grad_down = grads
    inward = adamw(inward_weight, grad_in, inward_first, inward_second, 0.05, 0.1)
    outward = adamw(outward_weight, grad_out, outward_first, outward_second, 0.05, 0.1)
    expand = adamw(expand_weight, grad_up, expand_first, expand_second, 0.05, 0.1)
    reduce_all = adamw(reduce_weight, grad_down, reduce_first, reduce_second, 0.05, 0.1)
    gains_all = adamw(norm_gains, grad_gains, gains_first, gains_second, 0.5, 0.0)
    taps_all = adamw(conv_taps, grad_taps, taps_first, taps_second, 0.5, 0.0)
    return (output.astype(jnp.bfloat16), grad_tokens, inward[0], inward[1], inward[2], outward[0], outward[1], outward[2], expand[0], expand[1], expand[2], reduce_all[0], reduce_all[1], reduce_all[2], gains_all[0], gains_all[1], gains_all[2], taps_all[0], taps_all[1], taps_all[2])
```

```python
import jax
import jax.numpy as jnp
from jax import lax
from jax.sharding import Mesh
from jax.sharding import PartitionSpec as P

STEP = 8
BF = jnp.bfloat16
F32 = jnp.float32
CHIPS = ("z", "yh", "x")
SEQ = ("z", "yh", "x", "core")


def shift(value, axis, steps):
    count = lax.axis_size(axis)
    return lax.ppermute(value, axis, [(i, (i + steps) % count) for i in range(count)])


def passed_along(value, steps):
    count = lax.axis_size(CHIPS)
    first, last = max(0, -steps), min(count, count - steps)
    return lax.ppermute(value, CHIPS, [(i, i + steps) for i in range(first, last)])


def dot(a, b, dims):
    return lax.dot_general(a, b, (dims, ((), ())), preferred_element_type=F32)


def row_scale(values):
    return lax.rsqrt(jnp.mean(values * values, axis=1, keepdims=True) + 1e-05)


def adamw(weight, grad, first, second, rate, decay):
    first_new = 0.9 * first + 0.1 * grad
    second_new = 0.95 * second + 0.05 * grad * grad
    step_size = first_new / (1.0 - 0.9**STEP) / (jnp.sqrt(second_new / (1.0 - 0.95**STEP)) + 1e-08)
    return (weight - rate * (step_size + decay * weight), first_new, second_new)


def gather_direct(block, axis):
    return [block, shift(block, axis, -1), shift(block, axis, 2), shift(block, axis, 1)]


def gather_ring(block, axis):
    half = block.shape[0] // 2
    left = shift(block, axis, 1)
    right = shift(block, axis, -1)
    low = shift(right[:half], axis, -1)
    high = shift(left[half:], axis, 1)
    return [block, right, jnp.concatenate([low, high], 0), left]


def add(*terms):
    total = terms[0].astype(F32)
    for term in terms[1:]:
        total = total + term.astype(F32)
    return total


def scatter_direct(pieces, axis):
    one = shift(pieces[1], axis, 1)
    three = shift(pieces[3], axis, -1)
    two = shift(pieces[2], axis, 2)
    return add(pieces[0], one, two, three)


def scatter_ring(pieces, axis):
    own, one, two, three = pieces
    half = two.shape[0] // 2
    low = shift(two[:half], axis, 1)
    high = shift(two[half:], axis, -1)
    one = jnp.concatenate([add(one[:half], low).astype(BF), one[half:]], 0)
    three = jnp.concatenate([three[:half], add(three[half:], high).astype(BF)], 0)
    return add(own, shift(one, axis, 1), shift(three, axis, -1))


def gather_rows(rows, order):
    cols = rows.shape[1]
    both = jnp.concatenate([rows, shift(rows, "yh", 1)], 0)
    if order == "zx":
        part = jnp.concatenate(gather_direct(both, "z"), 0)
        pieces = gather_ring(part, "x")
        whole = jnp.stack([p.reshape(4, 2, 32, cols) for p in pieces], 2)
    else:
        part = jnp.stack([p.reshape(2, 32, cols) for p in gather_direct(both, "x")], 1)
        pieces = gather_ring(part.reshape(256, cols), "z")
        whole = jnp.concatenate(pieces, 0)
    return whole.reshape(1024, cols)


def scatter_rows(pieces, order, core):
    cols = pieces[0].shape[1]
    if order == "xz":
        part = scatter_ring(pieces, "x").astype(BF).reshape(4, 64, cols)
        part = scatter_direct([part[i] for i in range(4)], "z")
    else:
        part = scatter_ring(pieces, "z").astype(BF).reshape(2, 4, 32, cols)
        part = scatter_direct([part[:, i].reshape(64, cols) for i in range(4)], "x")
    part = part.astype(BF)
    part = add(part[:32], shift(part[32:], "yh", 1))
    mine = jnp.where(core == 0, part[:16], part[16:])
    got = shift(jnp.where(core == 0, part[16:], part[:16]), "core", 1)
    return jnp.where(core == 0, mine, got), jnp.where(core == 0, got, mine)


def sum_small(value):
    for axis in ("core", "tp", "yh"):
        value = value + shift(value, axis, 1)
    for axis in ("x", "z"):
        one, two, three = shift(value, axis, 1), shift(value, axis, 2), shift(value, axis, -1)
        value = (value + two) + (one + three)
    return value


def group_sum(partial):
    partial = partial.astype(BF)
    own = add(partial[:256], shift(partial[256:], "core", 1)).astype(BF)
    return add(own, shift(own, "tp", 1))


def both_blocks(own):
    return jnp.concatenate([own, shift(own, "core", 1)], 0)


def body(
    tokens,
    cotangent,
    doc_ids,
    inward_weight,
    inward_first,
    inward_second,
    outward_weight,
    outward_first,
    outward_second,
    expand_weight,
    expand_first,
    expand_second,
    reduce_weight,
    reduce_first,
    reduce_second,
    norm_gains,
    gains_first,
    gains_second,
    conv_taps,
    taps_first,
    taps_second,
):
    z, yh, x = lax.axis_index("z"), lax.axis_index("yh"), lax.axis_index("x")
    core, tp = lax.axis_index("core"), lax.axis_index("tp")
    width = tokens.shape[1]
    chans = inward_weight.shape[2] // 2
    hidden = expand_weight.shape[2] // 2

    def split(weight):
        halves = weight.astype(BF).reshape(weight.shape[:-1] + (2, weight.shape[-1] // 2))
        mine = jnp.where(core == 0, halves[..., 0, :], halves[..., 1, :])
        theirs = jnp.where(core == 0, halves[..., 1, :], halves[..., 0, :])
        return mine.reshape(16, -1), theirs.reshape(16, -1)

    def chip_rows(weights):
        pairs = [split(w) for w in weights]
        mine = jnp.concatenate([p[0] for p in pairs], 1)
        got = shift(jnp.concatenate([p[1] for p in pairs], 1), "core", 1)
        first = jnp.where(core == 0, mine, got)
        second = jnp.where(core == 0, got, mine)
        return jnp.concatenate([first, second], 0)

    w_mixer = gather_rows(chip_rows([inward_weight, outward_weight]), "xz")
    w_up = gather_rows(chip_rows([expand_weight]), "zx")
    w_down = gather_rows(chip_rows([reduce_weight]), "xz")
    w_in, w_out = w_mixer[:, : 3 * chans], w_mixer[:, 3 * chans :]

    index = jnp.arange(width, dtype=jnp.int32)
    rel_z, rel_y, rel_x, low = index // 256, (index // 128) % 2, (index // 32) % 4, index % 32
    source = (((z + rel_z) % 4 * 2 + (yh + rel_y) % 2) * 4 + (x + rel_x) % 4) * 32 + low
    perm = (index[:, None] == source[None, :]).astype(BF)
    frame_zx = ((rel_y * 4 + rel_x) * 32 + low) + rel_z * 256
    swapped = (index // 256) * 32 + (index // 64) % 4 * 256 + (index // 32) % 2 * 128 + low
    perm_x = (frame_zx[:, None] == swapped[None, :]).astype(BF)
    exact = lax.Precision.HIGHEST

    gidx = (z * 2 + yh) * 4 + x
    first_doc, second_doc = doc_ids[2 * gidx], doc_ids[2 * gidx + 1]
    before = doc_ids[jnp.maximum(2 * gidx - 1, 0)]
    after = doc_ids[jnp.minimum(2 * gidx + 2, 63)]
    prev_same = ((gidx > 0) & (before == first_doc)).astype(F32)
    next_same = ((gidx < 31) & (after == second_doc)).astype(F32)
    inner_same = (first_doc == second_doc).astype(F32)

    tokens_rel = dot(tokens, perm, ((1,), (0,))).astype(BF)
    cot_rel = dot(cotangent, perm, ((1,), (0,))).astype(BF)
    gains = jnp.dot(norm_gains, perm.astype(F32), precision=exact)
    gain_one, gain_two = gains[0], gains[1]
    taps = jnp.where(core == 0, conv_taps[:, :chans], conv_taps[:, chans:])

    tokens_all = both_blocks(tokens_rel)
    cot_all = both_blocks(cot_rel)
    xf_all = tokens_all.astype(F32)
    scale_all = row_scale(xf_all)
    unit_all = xf_all * scale_all
    normed = (unit_all * gain_one).astype(BF)
    xf, scale_one = xf_all[:256], scale_all[:256]

    proj = dot(normed, w_in, ((1,), (0,)))
    part_b, part_c, part_x = proj[:, :chans], proj[:, chans : 2 * chans], proj[:, 2 * chans :]
    gated_in = (part_b * part_x).astype(BF)
    own_g, oth_g = gated_in[:256].astype(F32), gated_in[256:].astype(F32)
    halo = passed_along(jnp.where(core == 1, gated_in[254:256], gated_in[510:]), 1)
    halo = halo.astype(F32) * prev_same
    own_prev = jnp.where(core == 0, halo, oth_g[254:] * inner_same)
    oth_prev = jnp.where(core == 0, own_g[254:] * inner_same, halo)
    own_ext = jnp.concatenate([own_prev, own_g], 0)
    oth_ext = jnp.concatenate([oth_prev, oth_g], 0)
    back_two = jnp.concatenate([own_ext[:256], oth_ext[:256]], 0)
    back_one = jnp.concatenate([own_ext[1:257], oth_ext[1:257]], 0)
    gated_f = gated_in.astype(F32)
    mixed = taps[2] * gated_f + taps[1] * back_one + taps[0] * back_two
    gated_out = (part_c * mixed).astype(BF)
    resid = xf + group_sum(dot(gated_out, w_out, ((1,), (1,))))
    scale_two = row_scale(resid)
    normed_two = both_blocks((resid * scale_two * gain_two).astype(BF))
    normed_two_x = dot(normed_two, perm_x, ((1,), (0,))).astype(BF)

    gate_up = dot(normed_two, w_up, ((1,), (0,)))
    gate, upper = gate_up[:, :hidden], gate_up[:, hidden:]
    sigma = jax.nn.sigmoid(gate)
    silu = gate * sigma
    act = (silu * upper).astype(BF)
    dact = dot(cot_all, w_down, ((1,), (0,)))
    dgu = jnp.concatenate(
        [dact * upper * sigma * (1.0 + gate * (1.0 - sigma)), dact * silu], 1
    ).astype(BF)
    dnormed_two = group_sum(dot(dgu, w_up, ((1,), (1,))))
    down_pieces = [
        dot(cot_all[:, 256 * i : 256 * (i + 1)], act, ((0,), (0,))).astype(BF) for i in range(4)
    ]
    up_pieces = [
        dot(normed_two_x[:, 256 * i : 256 * (i + 1)], dgu, ((0,), (0,))).astype(BF)
        for i in range(4)
    ]
    grad_down = scatter_rows(down_pieces, "zx", core)
    grad_up = scatter_rows(up_pieces, "xz", core)
    block_rel = (resid + group_sum(dot(act, w_down, ((1,), (1,))))).astype(BF)
    block_out = dot(block_rel, perm, ((1,), (1,))).astype(BF)

    q_two = dnormed_two * gain_two
    dresid = (
        cot_rel.astype(F32)
        + scale_two * q_two
        - resid * scale_two**3 * jnp.mean(q_two * resid, axis=1, keepdims=True)
    )
    dgain_two = jnp.sum(dnormed_two * resid * scale_two, axis=0)

    dattn = both_blocks(dresid.astype(BF))
    dgated_out = dot(dattn, w_out, ((1,), (0,)))
    dpart_c = dgated_out * mixed
    dmixed = dgated_out * part_c
    own_d, oth_d = dmixed[:256], dmixed[256:]
    halo_back = passed_along(jnp.where(core == 0, own_d[:2], oth_d[:2]), -1) * next_same
    own_next = jnp.where(core == 0, oth_d[:2] * inner_same, halo_back)
    oth_next = jnp.where(core == 0, halo_back, own_d[:2] * inner_same)
    own_dext = jnp.concatenate([own_d, own_next], 0)
    oth_dext = jnp.concatenate([oth_d, oth_next], 0)
    dgated_in = (
        taps[2] * dmixed
        + taps[1] * jnp.concatenate([own_dext[1:257], oth_dext[1:257]], 0)
        + taps[0] * jnp.concatenate([own_dext[2:], oth_dext[2:]], 0)
    )
    dtaps = jnp.stack(
        [
            jnp.sum(dmixed * back_two, axis=0),
            jnp.sum(dmixed * back_one, axis=0),
            jnp.sum(dmixed * gated_f, axis=0),
        ],
        0,
    )
    dproj = jnp.concatenate([dgated_in * part_x, dpart_c, dgated_in * part_b], 1).astype(BF)
    mixer_pieces = [
        jnp.concatenate(
            [
                dot(normed[:, 256 * i : 256 * (i + 1)], dproj, ((0,), (0,))).astype(BF),
                dot(dattn[:, 256 * i : 256 * (i + 1)], gated_out, ((0,), (0,))).astype(BF),
            ],
            1,
        )
        for i in range(4)
    ]
    grad_mixer = scatter_rows(mixer_pieces, "zx", core)

    dnormed_part = dot(dproj, w_in, ((1,), (1,)))
    dgain_one = jnp.sum(dnormed_part * unit_all, axis=0)
    dgains = jnp.stack([dgain_one, jnp.where(tp == 0, dgain_two, 0.0)], 0)
    dgains = lax.dot_general(
        dgains, perm.astype(F32), (((1,), (1,)), ((), ())), precision=exact
    )
    place = jnp.arange(4, dtype=jnp.int32)[None, :, None] == tp * 2 + core
    dtaps_wide = jnp.where(place, dtaps[:, None, :], 0.0).reshape(3, width)
    small = sum_small(jnp.concatenate([dgains, dtaps_wide], 0))
    grad_gains = small[:2]
    half = width // 2
    grad_taps = jnp.where(tp == 0, small[2:, :half], small[2:, half:])

    dnormed = group_sum(dnormed_part)
    q_one = dnormed * gain_one
    grad_rel = (
        dresid + scale_one * q_one - xf * scale_one**3 * jnp.mean(q_one * xf, axis=1, keepdims=True)
    )
    grad_tokens = lax.dot_general(
        grad_rel, perm.astype(F32), (((1,), (1,)), ((), ())), precision=exact
    )

    def joined(pair, first, last, shape):
        parts = [p[:, first:last].reshape(shape[:-1] + (1, shape[-1])) for p in pair]
        return jnp.concatenate(parts, len(shape) - 1).reshape(shape[:-1] + (2 * shape[-1],))

    grad_in = joined(grad_mixer, 0, 3 * chans, (16, 3, chans))
    grad_out = joined(grad_mixer, 3 * chans, 4 * chans, (16, chans))
    grad_up = joined(grad_up, 0, 2 * hidden, (16, 2, hidden))
    grad_down = joined(grad_down, 0, hidden, (16, hidden))
    return (
        block_out,
        grad_tokens,
        *adamw(inward_weight, grad_in, inward_first, inward_second, 0.05, 0.1),
        *adamw(outward_weight, grad_out, outward_first, outward_second, 0.05, 0.1),
        *adamw(expand_weight, grad_up, expand_first, expand_second, 0.05, 0.1),
        *adamw(reduce_weight, grad_down, reduce_first, reduce_second, 0.05, 0.1),
        *adamw(norm_gains, grad_gains, gains_first, gains_second, 0.5, 0.0),
        *adamw(conv_taps, grad_taps, taps_first, taps_second, 0.5, 0.0),
    )


def solution(mesh):
    fine = Mesh(mesh.devices.reshape(4, 2, 4, 2, 2), ("z", "yh", "x", "core", "tp"))
    rows = P(SEQ, None)
    wide, flat, tap = P(SEQ, None, "tp"), P(SEQ, "tp"), P(None, "tp")
    weights = (wide,) * 3 + (flat,) * 3 + (wide,) * 3 + (flat,) * 3
    small = (P(),) * 3 + (tap,) * 3
    return jax.shard_map(
        body,
        mesh=fine,
        in_specs=(rows, rows, P()) + weights + small,
        out_specs=(rows, rows) + weights + small,
        check_vma=False,
    )
```

```python
import jax
import jax.numpy as jnp
from jax import lax
from jax.sharding import Mesh
from jax.sharding import PartitionSpec as P

STEP = 8
BF = jnp.bfloat16
F32 = jnp.float32
CHIPS = ("z", "yh", "x")
SEQ = ("z", "yh", "x", "core")


def shift(value, axis, steps):
    count = lax.axis_size(axis)
    return lax.ppermute(value, axis, [(i, (i + steps) % count) for i in range(count)])


def passed_along(value, steps):
    count = lax.axis_size(CHIPS)
    first, last = max(0, -steps), min(count, count - steps)
    return lax.ppermute(value, CHIPS, [(i, i + steps) for i in range(first, last)])


def dot(a, b, dims):
    return lax.dot_general(a, b, (dims, ((), ())), preferred_element_type=F32)


def row_scale(values):
    return lax.rsqrt(jnp.mean(values * values, axis=1, keepdims=True) + 1e-05)


def adamw(weight, grad, first, second, rate, decay):
    first_new = 0.9 * first + 0.1 * grad
    second_new = 0.95 * second + 0.05 * grad * grad
    step_size = first_new / (1.0 - 0.9**STEP) / (jnp.sqrt(second_new / (1.0 - 0.95**STEP)) + 1e-08)
    return (weight - rate * (step_size + decay * weight), first_new, second_new)


def gather_direct(block, axis):
    return [block, shift(block, axis, -1), shift(block, axis, 2), shift(block, axis, 1)]


def gather_ring(block, axis, before=None):
    half = block.shape[0] // 2
    left = shift(block, axis, 1)
    right = shift(block, axis, -1)
    low = shift(after(right[:half], before), axis, -1)
    high = shift(after(left[half:], before), axis, 1)
    return [block, right, jnp.concatenate([low, high], 0), left], right


def add(*terms):
    total = terms[0].astype(F32)
    for term in terms[1:]:
        total = total + term.astype(F32)
    return total


def scatter_direct(pieces, axis):
    one = shift(pieces[1], axis, 1)
    three = shift(pieces[3], axis, -1)
    two = shift(pieces[2], axis, 2)
    return add(pieces[0], one, two, three)


def scatter_ring(pieces, axis, before=None):
    own, one, two, three = pieces
    half = two.shape[0] // 32 * 16
    low = shift(two[:half], axis, 1)
    high = shift(two[half:], axis, -1)
    one = jnp.concatenate([after(add(one[:half], low), before).astype(BF), one[half:]], 0)
    three = jnp.concatenate([three[:half], after(add(three[half:], high), before).astype(BF)], 0)
    return add(own, shift(one, axis, 1), shift(three, axis, -1)), one


def gather_rows(rows, order, before=None):
    cols = rows.shape[1]
    if order == "xz":
        part = jnp.stack([p.reshape(2, 32, cols) for p in gather_direct(rows, "x")], 1)
        pieces, step = gather_ring(part.reshape(256, cols), "z", before)
        return jnp.concatenate(pieces, 0), step
    part = jnp.concatenate(gather_direct(rows, "z"), 0)
    pieces, step = gather_ring(part, "x", before)
    return jnp.stack([p.reshape(4, 2, 32, cols) for p in pieces], 2).reshape(1024, cols), step


def scatter_second(part, axis, before=None):
    cols = part.shape[1]
    part = after(part, before).astype(BF)
    if axis == "x":
        blocks = part[:256].reshape(2, 4, 32, cols)
        pieces = [blocks[:, i].reshape(64, cols) for i in range(4)]
    else:
        pieces = [part[64 * i : 64 * (i + 1)] for i in range(4)]
    if part.shape[0] > 256:
        pieces = [jnp.concatenate([piece, part[256:]], 0) for piece in pieces]
    return scatter_direct(pieces, axis)


def swap_diagonal(value):
    return lax.ppermute(value, ("yh", "core"), [(i, 3 - i) for i in range(4)])


def by_core(core, own, other):
    return jnp.where(core == 0, own, other), jnp.where(core == 0, other, own)


def gather_pair(mine, theirs, core, before=None):
    mine, theirs = after(mine, before), after(theirs, before)
    here = by_core(core, mine, shift(theirs, "core", 1))
    there = by_core(core, shift(mine, "yh", 1), swap_diagonal(theirs))
    return jnp.concatenate(here + there, 0)


def scatter_pair(part, small, core):
    part, small = part.astype(BF), small.astype(BF)
    here, there = part[:32], part[32:]

    def pick(rows, own):
        first, second = (rows[:16], rows[16:]) if own else (rows[16:], rows[:16])
        return jnp.concatenate([jnp.where(core == 0, first, second), small], 0)

    got = shift(pick(there, True), "yh", 1)
    got_core = shift(pick(here, False), "core", 1)
    got_diagonal = swap_diagonal(pick(there, False))
    own = add(pick(here, True), got)
    other = add(got_core, got_diagonal)
    return by_core(core, own[:16], other[:16]), own[16:] + other[16:]


OWN, BOTH = 256, 512


def core_sum(partial):
    partial = partial.astype(BF)
    extra = partial[BOTH:]
    got = shift(jnp.concatenate([partial[OWN:BOTH], extra], 0), "core", 1)
    return add(jnp.concatenate([partial[:OWN], extra], 0), got).astype(BF)


def pair_sum(own):
    return add(own, shift(own, "tp", 1))


def both_blocks(own):
    return jnp.concatenate([own[:OWN], shift(own[:OWN], "core", 1), own[OWN:]], 0)


def after(value, before):
    if before is None:
        return value
    corner = before[tuple(slice(0, 1) for _ in before.shape)].reshape((1,) * value.ndim)
    if value.dtype == jnp.int32:
        return value + (corner.astype(F32) > 3e38).astype(jnp.int32)
    return value + corner.astype(value.dtype) * 0


def body(
    tokens,
    cotangent,
    doc_ids,
    inward_weight,
    inward_first,
    inward_second,
    outward_weight,
    outward_first,
    outward_second,
    expand_weight,
    expand_first,
    expand_second,
    reduce_weight,
    reduce_first,
    reduce_second,
    norm_gains,
    gains_first,
    gains_second,
    conv_taps,
    taps_first,
    taps_second,
):
    z, yh, x = lax.axis_index("z"), lax.axis_index("yh"), lax.axis_index("x")
    core, tp = lax.axis_index("core"), lax.axis_index("tp")
    width = tokens.shape[1]
    chans = inward_weight.shape[2] // 2
    hidden = expand_weight.shape[2] // 2

    def split(weight):
        halves = weight.astype(BF).reshape(weight.shape[:-1] + (2, weight.shape[-1] // 2))
        pair = by_core(core, halves[..., 0, :], halves[..., 1, :])
        return [p.reshape(16, -1) for p in pair]

    quarters = zip(*[split(w) for w in (expand_weight, inward_weight, outward_weight, reduce_weight)])
    all_pair = gather_pair(*[jnp.concatenate(q, 1) for q in quarters], core)
    cuts = (2 * hidden, 2 * hidden + 4 * chans)
    up_pair, mixer_pair, down_pair = jnp.split(all_pair, cuts, axis=1)
    w_up = lax.all_gather(up_pair, ("z", "x"), axis=0, tiled=True)

    index = jnp.arange(width, dtype=jnp.int32)
    low = index % 32
    rel_z, rel_y, rel_x = (z + index // 256) % 4, (yh + index // 128) % 2, (x + index // 32) % 4
    relative = ((rel_z * 2 + rel_y) * 4 + rel_x) * 32 + low
    pair = ((index // 256 * 2 + (yh + index // 32) % 2) * 4 + index // 64 % 4) * 32 + low
    perm = (index[:, None] == relative[None, :]).astype(BF)
    swapped = (index // 64 % 4 * 8 + index // 32 % 2 * 4 + index // 256) * 32 + low
    perm_x = (index[:, None] == swapped[None, :]).astype(BF)
    perm_pair = (relative[:, None] == pair[None, :]).astype(BF)
    exact = lax.Precision.HIGHEST

    gidx = (z * 2 + yh) * 4 + x
    first_doc, second_doc = doc_ids[2 * gidx], doc_ids[2 * gidx + 1]
    doc_before = doc_ids[jnp.maximum(2 * gidx - 1, 0)]
    doc_after = doc_ids[jnp.minimum(2 * gidx + 2, 63)]
    doc_before = jnp.where(gidx > 0, doc_before, -1)
    doc_after = jnp.where(gidx < 31, doc_after, -2)

    row = jnp.arange(BOTH + 16, dtype=jnp.int32)
    token = jnp.where(row < OWN, row + core * OWN, row - core * OWN)
    token = jnp.where(row < BOTH, token, jnp.where(row < BOTH + 8, row - BOTH - 8, row - 8))
    doc = jnp.where(token < OWN, first_doc, second_doc)
    doc = jnp.where(token < 0, doc_before, jnp.where(token < BOTH, doc, doc_after))
    gap = token[:, None] - token[None, :]
    same = doc[:, None] == doc[None, :]
    shifts = jnp.concatenate([(gap == k) & same for k in (1, 2)], 0).astype(BF)

    edge = jnp.concatenate(
        [
            jnp.where(core == 1, tokens[-8:], tokens[:8]),
            jnp.where(core == 1, cotangent[-8:], cotangent[:8]),
        ],
        0,
    )
    swaps = [(2 * g + 1, 2 * g + 2) for g in range(31)]
    edge = lax.ppermute(edge, SEQ, swaps + [(b, a) for a, b in swaps])
    rows = jnp.concatenate([tokens, cotangent, edge], 0)
    rows = dot(rows, perm, ((1,), (0,))).astype(BF)
    got = shift(rows, "core", 1)
    edge, got_edge = rows[BOTH:], got[BOTH:]
    edges = jnp.where(core == 0, edge, got_edge), jnp.where(core == 0, got_edge, edge)
    tokens_all = jnp.concatenate([rows[:OWN], got[:OWN], edges[0][:8], edges[1][:8]], 0)
    cot_all = jnp.concatenate([rows[OWN:BOTH], got[OWN:BOTH], edges[0][8:], edges[1][8:]], 0)
    cot_x = dot(cot_all[:BOTH], perm_x, ((1,), (0,))).astype(BF)
    gains = jnp.dot(norm_gains, perm.astype(F32), precision=exact)
    gain_one, gain_two = gains[0], gains[1]
    taps = jnp.where(core == 0, conv_taps[:, :chans], conv_taps[:, chans:])

    def own_rows(values):
        return jnp.concatenate([values[:OWN], values[BOTH:]], 0)

    def columns(values, i):
        return values[:BOTH, 256 * i : 256 * (i + 1)]

    xf_all = tokens_all.astype(F32)
    scale_all = row_scale(xf_all)
    unit_all = xf_all * scale_all
    normed = lax.optimization_barrier((unit_all * gain_one).astype(BF))
    xf, scale_one = own_rows(xf_all), scale_all[:OWN]

    w_mixer, step = gather_rows(mixer_pair, "xz", normed)
    w_in, w_out = w_mixer[:, : 3 * chans], w_mixer[:, 3 * chans :]
    proj = dot(normed, w_in, ((1,), (0,)))
    part_b, part_c, part_x = proj[:, :chans], proj[:, chans : 2 * chans], proj[:, 2 * chans :]
    gated_in = (part_b * part_x).astype(BF)
    back = dot(shifts, gated_in, ((1,), (0,)))
    back_one, back_two = back[: BOTH + 16], back[BOTH + 16 :]
    mixed = taps[2] * gated_in.astype(F32) + taps[1] * back_one + taps[0] * back_two
    gated_out = (part_c * mixed).astype(BF)
    mixer_sum = core_sum(dot(gated_out, w_out, ((1,), (1,))))
    w_down, _ = gather_rows(after(down_pair, step), "zx", mixer_sum)
    resid = xf + pair_sum(mixer_sum)
    scale_two = row_scale(resid)
    normed_two = (resid * scale_two * gain_two).astype(BF)
    normed_two = both_blocks(dot(normed_two, perm_pair, ((1,), (0,))).astype(BF))
    normed_two = lax.optimization_barrier(normed_two)

    dact = dot(cot_all, w_down, ((1,), (0,)))
    gate_up = dot(normed_two, w_up, ((1,), (0,)))
    gate, upper = gate_up[:, :hidden], gate_up[:, hidden:]
    sigma = jax.nn.sigmoid(gate)
    silu = gate * sigma
    act = (silu * upper).astype(BF)
    dgu = jnp.concatenate(
        [dact * upper * sigma * (1.0 + gate * (1.0 - sigma)), dact * silu], 1
    ).astype(BF)
    dgu, act = lax.optimization_barrier((dgu, act))
    grad_up_whole = dot(normed_two[:BOTH], dgu[:BOTH], ((0,), (0,))).astype(BF)
    grad_up = lax.psum_scatter(grad_up_whole, ("z", "x"), scatter_dimension=0, tiled=True)
    dnormed_two = core_sum(dot(dgu, w_up, ((1,), (1,))))
    dnormed_two = dot(dnormed_two, perm_pair, ((1,), (1,))).astype(BF)
    act_later = after(act[:BOTH], dnormed_two)
    down_pieces = [dot(columns(cot_x, i), act_later, ((0,), (0,))).astype(BF) for i in range(4)]
    block_part = dot(act_later, w_down, ((1,), (1,)))
    dnormed_two = pair_sum(dnormed_two)

    cot_own = own_rows(cot_all).astype(F32)
    q_two = dnormed_two * gain_two
    dresid = (
        cot_own
        + scale_two * q_two
        - resid * scale_two**3 * jnp.mean(q_two * resid, axis=1, keepdims=True)
    )
    dgain_two = jnp.sum((dnormed_two * resid * scale_two)[:OWN], axis=0)

    dattn_own = dresid.astype(BF)
    dattn = both_blocks(dattn_own)
    grad_down, _ = scatter_ring(down_pieces, "x", dattn[OWN:])
    dgated_out = dot(dattn, w_out, ((1,), (0,)))
    dpart_c = (dgated_out * mixed)[:BOTH]
    dmixed = dgated_out * part_c
    tapped = jnp.concatenate([taps[1] * dmixed, taps[0] * dmixed], 0)
    high = tapped.astype(BF)
    lower = (tapped - high.astype(F32)).astype(BF)
    ahead = dot(shifts, high, ((0,), (0,))) + dot(shifts, lower, ((0,), (0,)))
    dmixed = dmixed[:BOTH]
    dgated_in = taps[2] * dmixed + ahead[:BOTH]
    dtaps = jnp.stack(
        [
            jnp.sum(dmixed * back_two[:BOTH], axis=0),
            jnp.sum(dmixed * back_one[:BOTH], axis=0),
            jnp.sum(dmixed * gated_in[:BOTH].astype(F32), axis=0),
        ],
        0,
    )
    dproj = jnp.concatenate(
        [dgated_in * part_x[:BOTH], dpart_c, dgated_in * part_b[:BOTH]], 1
    ).astype(BF)
    dproj = lax.optimization_barrier(dproj)

    dnormed_part = dot(dproj, w_in, ((1,), (1,)))
    dgain_one = jnp.sum(dnormed_part * unit_all[:BOTH], axis=0)
    dgains = jnp.stack([dgain_one, jnp.where(tp == 0, dgain_two, 0.0)], 0)
    dgains = lax.dot_general(dgains, perm.astype(F32), (((1,), (1,)), ((), ())), precision=exact)
    place = jnp.arange(4, dtype=jnp.int32)[None, :, None] == tp * 2 + core
    dtaps_wide = jnp.where(place, dtaps[:, None, :], 0.0).reshape(3, width)
    small = jnp.concatenate([dgains, dtaps_wide, jnp.zeros((11, width), F32)], 0).astype(BF)
    mixer_pieces = [
        jnp.concatenate(
            [
                jnp.concatenate(
                    [
                        dot(columns(normed, i), dproj, ((0,), (0,))).astype(BF),
                        dot(columns(dattn, i), gated_out[:BOTH], ((0,), (0,))).astype(BF),
                    ],
                    1,
                ),
                small,
            ],
            0,
        )
        for i in range(4)
    ]
    grad_mixer, second_step = scatter_ring(mixer_pieces, "z")
    grad_down = scatter_second(grad_down, "z", grad_mixer)
    grad_mixer = scatter_second(grad_mixer, "x")
    grads = jnp.concatenate([grad_up, grad_mixer[:64].astype(BF), grad_down.astype(BF)], 1)
    small = jnp.pad(grad_mixer[64:69].reshape(1, -1), ((0, 0), (0, 2 * grads.shape[1] - 5 * width)))
    grads, small = scatter_pair(grads, small.reshape(2, grads.shape[1]), core)
    small = small.reshape(-1)[: 5 * width].reshape(5, width)
    small = small + shift(small, "tp", 1)
    grad_gains = small[:2]
    half = width // 2
    grad_taps = jnp.where(tp == 0, small[2:, :half], small[2:, half:])

    parts = [dnormed_part.astype(BF), block_part.astype(BF)]
    got = jnp.concatenate([p[OWN:BOTH] for p in parts], 0)
    got = shift(after(got, second_step), "core", 1)
    sums = pair_sum(add(jnp.concatenate([p[:OWN] for p in parts], 0), got).astype(BF))
    dnormed = sums[:OWN]
    block_rel = (resid[:OWN] + sums[OWN:]).astype(BF)
    block_out = dot(block_rel, perm, ((1,), (1,))).astype(BF)

    q_one = dnormed * gain_one
    xf = xf[:OWN]
    grad_rel = (
        dresid[:OWN]
        + scale_one * q_one
        - xf * scale_one**3 * jnp.mean(q_one * xf, axis=1, keepdims=True)
    )
    high = grad_rel.astype(BF)
    lower = (grad_rel - high.astype(F32)).astype(BF)
    grad_tokens = dot(high, perm, ((1,), (1,))) + dot(lower, perm, ((1,), (1,)))

    def joined(pair, first, last, shape):
        parts = [p[:, first:last].reshape(shape[:-1] + (1, shape[-1])) for p in pair]
        return jnp.concatenate(parts, len(shape) - 1).reshape(shape[:-1] + (2 * shape[-1],))

    ends = [2 * hidden, 2 * hidden + 3 * chans, 2 * hidden + 4 * chans, 3 * hidden + 4 * chans]
    grad_up = joined(grads, 0, ends[0], (16, 2, hidden))
    grad_in = joined(grads, ends[0], ends[1], (16, 3, chans))
    grad_out = joined(grads, ends[1], ends[2], (16, chans))
    grad_down = joined(grads, ends[2], ends[3], (16, hidden))
    return (
        block_out,
        grad_tokens,
        *adamw(inward_weight, grad_in, inward_first, inward_second, 0.05, 0.1),
        *adamw(outward_weight, grad_out, outward_first, outward_second, 0.05, 0.1),
        *adamw(expand_weight, grad_up, expand_first, expand_second, 0.05, 0.1),
        *adamw(reduce_weight, grad_down, reduce_first, reduce_second, 0.05, 0.1),
        *adamw(norm_gains, grad_gains, gains_first, gains_second, 0.5, 0.0),
        *adamw(conv_taps, grad_taps, taps_first, taps_second, 0.5, 0.0),
    )


def solution(mesh):
    fine = Mesh(mesh.devices.reshape(4, 2, 4, 2, 2), ("z", "yh", "x", "core", "tp"))
    rows = P(SEQ, None)
    wide, flat, tap = P(SEQ, None, "tp"), P(SEQ, "tp"), P(None, "tp")
    weights = (wide,) * 3 + (flat,) * 3 + (wide,) * 3 + (flat,) * 3
    small = (P(),) * 3 + (tap,) * 3
    return jax.shard_map(
        body,
        mesh=fine,
        in_specs=(rows, rows, P()) + weights + small,
        out_specs=(rows, rows) + weights + small,
        check_vma=False,
    )
```

```python
import jax
import jax.numpy as jnp
from jax import lax
from jax.experimental import pallas as pl
from jax.experimental.pallas import tpu as pltpu
from jax.sharding import Mesh
from jax.sharding import PartitionSpec as P

STEP = 8
BF = jnp.bfloat16
F32 = jnp.float32
SEQ = ("z", "yh", "x", "core")


def shift(value, axis, steps):
    count = lax.axis_size(axis)
    return lax.ppermute(value, axis, [(i, (i + steps) % count) for i in range(count)])


def dot(a, b, dims):
    return lax.dot_general(a, b, (dims, ((), ())), preferred_element_type=F32)


def row_scale(values):
    return lax.rsqrt(jnp.mean(values * values, axis=1, keepdims=True) + 1e-05)


def adamw(weight, grad, first, second, rate, decay):
    first_new = 0.9 * first + 0.1 * grad
    second_new = 0.95 * second + 0.05 * grad * grad
    step_size = first_new / (1.0 - 0.9**STEP) / (jnp.sqrt(second_new / (1.0 - 0.95**STEP)) + 1e-08)
    return (weight - rate * (step_size + decay * weight), first_new, second_new)


def gather_direct(block, axis):
    return [block, shift(block, axis, -1), shift(block, axis, 2), shift(block, axis, 1)]


def gather_ring(block, axis):
    half = block.shape[0] // 2
    left = shift(block, axis, 1)
    right = shift(block, axis, -1)
    low = shift(right[:half], axis, -1)
    high = shift(left[half:], axis, 1)
    return [block, right, jnp.concatenate([low, high], 0), left]


def add(*terms):
    total = terms[0].astype(F32)
    for term in terms[1:]:
        total = total + term.astype(F32)
    return total


def scatter_direct(pieces, axis):
    one = shift(pieces[1], axis, 1)
    three = shift(pieces[3], axis, -1)
    two = shift(pieces[2], axis, 2)
    return add(pieces[0], one, two, three)


def scatter_ring(pieces, axis, before):
    own, one, two, three = pieces
    half = two.shape[0] // 32 * 16
    low = shift(two[:half], axis, 1)
    high = shift(two[half:], axis, -1)
    one = jnp.concatenate([after(add(one[:half], low), before).astype(BF), one[half:]], 0)
    three = jnp.concatenate([three[:half], after(add(three[half:], high), before).astype(BF)], 0)
    return add(own, shift(one, axis, 1), shift(three, axis, -1))


def gather_rows(rows):
    cols = rows.shape[1]
    part = jnp.stack([p.reshape(2, 32, cols) for p in gather_direct(rows, "x")], 1)
    pieces = gather_ring(part.reshape(256, cols), "z")
    return jnp.concatenate(pieces, 0), pieces[1]


def scatter_second(part):
    cols = part.shape[1]
    part = part.astype(BF)
    blocks = part[:256].reshape(2, 4, 32, cols)
    pieces = [jnp.concatenate([blocks[:, i].reshape(64, cols), part[256:]], 0) for i in range(4)]
    return scatter_direct(pieces, "x")


def swap_diagonal(value):
    return lax.ppermute(value, ("yh", "core"), [(i, 3 - i) for i in range(4)])


def halved(value):
    high = value.astype(BF)
    return high, (value - high.astype(F32)).astype(BF)


def by_core(core, own, other):
    return jnp.where(core == 0, own, other), jnp.where(core == 0, other, own)


def gather_pair(mine, theirs, core):
    got = shift(theirs, "core", 1)
    here = by_core(core, mine, got)
    there = by_core(core, shift(mine, "yh", 1), swap_diagonal(theirs))
    return jnp.concatenate(here + there, 0), got


def scatter_pair(part, small, core):
    part, small = part.astype(BF), small.astype(BF)
    here, there = part[:32], part[32:]

    def pick(rows, own):
        first, second = (rows[:16], rows[16:]) if own else (rows[16:], rows[:16])
        return jnp.concatenate([jnp.where(core == 0, first, second), small], 0)

    got = shift(pick(there, True), "yh", 1)
    got_core = shift(pick(here, False), "core", 1)
    got_diagonal = swap_diagonal(pick(there, False))
    own = add(pick(here, True), got)
    other = add(got_core, got_diagonal)
    return by_core(core, own[:16], other[:16]), own[16:] + other[16:]


OWN, BOTH = 256, 512


def core_sum(partial):
    partial = partial.astype(BF)
    extra = partial[BOTH:]
    got = shift(jnp.concatenate([partial[OWN:BOTH], extra], 0), "core", 1)
    return add(jnp.concatenate([partial[:OWN], extra], 0), got).astype(BF)


def pair_sum(own):
    return add(own, shift(own, "tp", 1))


def both_blocks(own):
    return jnp.concatenate([own[:OWN], shift(own[:OWN], "core", 1), own[OWN:]], 0)


def feed_forward_kernel(
    normed_ref, cot_ref, weights_ref, grads_ref, dnormed_ref, block_ref, held, sums, came, left
):
    cols = held.shape[2]
    span = [pl.ds(k * cols, cols) for k in range(3)]
    arriving = [
        pltpu.make_async_copy(weights_ref.at[:, span[k]], held.at[k], came.at[k]) for k in range(3)
    ]
    leaving = [
        pltpu.make_async_copy(sums.at[k], grads_ref.at[:, span[k]], left.at[k]) for k in range(3)
    ]
    for k in (2, 0, 1):
        arriving[k].start()
    arriving[2].wait()
    dact = dot(cot_ref[...], held[2], ((1,), (0,)))
    arriving[0].wait()
    gate = dot(normed_ref[...], held[0], ((1,), (0,)))
    arriving[1].wait()
    upper = dot(normed_ref[...], held[1], ((1,), (0,)))
    sigma = jax.nn.sigmoid(gate)
    silu = gate * sigma
    act = (silu * upper).astype(BF)
    dgate = (dact * upper * sigma * (1.0 + gate * (1.0 - sigma))).astype(BF)
    dupper = (dact * silu).astype(BF)
    normed, cot = normed_ref[:BOTH], cot_ref[:BOTH]
    for k, rows, grad in ((0, normed, dgate), (1, normed, dupper), (2, cot, act)):
        sums[k] = dot(rows, grad[:BOTH], ((0,), (0,))).astype(BF)
        leaving[k].start()
    dnormed = dot(dgate, held[0], ((1,), (1,))) + dot(dupper, held[1], ((1,), (1,)))
    dnormed_ref[...] = dnormed.astype(BF)
    block_ref[...] = dot(act[:BOTH], held[2], ((1,), (1,))).astype(BF)
    for copy in leaving:
        copy.wait()


def feed_forward(normed, cot, weights):
    rows, width = normed.shape
    cols = weights.shape[1] // 3
    vmem, hbm = pl.BlockSpec(memory_space=pltpu.VMEM), pl.BlockSpec(memory_space=pl.ANY)
    return pl.pallas_call(
        feed_forward_kernel,
        in_specs=[vmem, vmem, hbm],
        out_specs=[hbm, vmem, vmem],
        out_shape=[
            jax.ShapeDtypeStruct(weights.shape, BF),
            jax.ShapeDtypeStruct((rows, width), BF),
            jax.ShapeDtypeStruct((BOTH, width), BF),
        ],
        scratch_shapes=[
            pltpu.VMEM((3, width, cols), BF),
            pltpu.VMEM((3, width, cols), BF),
            pltpu.SemaphoreType.DMA((3,)),
            pltpu.SemaphoreType.DMA((3,)),
        ],
        compiler_params=pltpu.CompilerParams(vmem_limit_bytes=48 * 2**20),
        cost_estimate=pl.CostEstimate(
            flops=18 * rows * width * cols,
            bytes_accessed=4 * weights.size,
            transcendentals=rows * cols,
        ),
    )(normed, cot, weights)


def after(value, before):
    if before is None:
        return value
    corner = before[tuple(slice(0, 1) for _ in before.shape)].reshape((1,) * value.ndim)
    if value.dtype == jnp.int32:
        return value + (corner.astype(F32) > 3e38).astype(jnp.int32)
    return value + corner.astype(value.dtype) * 0


def body(
    tokens,
    cotangent,
    doc_ids,
    inward_weight,
    inward_first,
    inward_second,
    outward_weight,
    outward_first,
    outward_second,
    expand_weight,
    expand_first,
    expand_second,
    reduce_weight,
    reduce_first,
    reduce_second,
    norm_gains,
    gains_first,
    gains_second,
    conv_taps,
    taps_first,
    taps_second,
):
    z, yh, x = lax.axis_index("z"), lax.axis_index("yh"), lax.axis_index("x")
    core, tp = lax.axis_index("core"), lax.axis_index("tp")
    width = tokens.shape[1]
    chans = inward_weight.shape[2] // 2
    hidden = expand_weight.shape[2] // 2

    def split(weight):
        halves = weight.astype(BF).reshape(weight.shape[:-1] + (2, weight.shape[-1] // 2))
        pair = by_core(core, halves[..., 0, :], halves[..., 1, :])
        return [p.reshape(16, -1) for p in pair]

    quarters = zip(*[split(w) for w in (expand_weight, reduce_weight, inward_weight, outward_weight)])
    all_pair, first_got = gather_pair(*[jnp.concatenate(q, 1) for q in quarters], core)
    feed_pair, mixer_pair = all_pair[:, : 3 * hidden], all_pair[:, 3 * hidden :]
    w_feed = lax.all_gather(feed_pair, ("z", "x"), axis=0, tiled=True)
    w_mixer, first_step = gather_rows(mixer_pair)

    index = after(jnp.arange(width, dtype=jnp.int32), first_step)
    low = index % 32
    rel_z, rel_y, rel_x = (z + index // 256) % 4, (yh + index // 128) % 2, (x + index // 32) % 4
    relative = ((rel_z * 2 + rel_y) * 4 + rel_x) * 32 + low
    pair = ((index // 256 * 2 + (yh + index // 32) % 2) * 4 + index // 64 % 4) * 32 + low
    perm = (index[:, None] == relative[None, :]).astype(BF)
    perm_pair = (relative[:, None] == pair[None, :]).astype(BF)
    exact = lax.Precision.HIGHEST

    gidx = (z * 2 + yh) * 4 + x
    first_doc, second_doc = doc_ids[2 * gidx], doc_ids[2 * gidx + 1]
    doc_before = doc_ids[jnp.maximum(2 * gidx - 1, 0)]
    doc_after = doc_ids[jnp.minimum(2 * gidx + 2, 63)]
    doc_before = jnp.where(gidx > 0, doc_before, -1)
    doc_after = jnp.where(gidx < 31, doc_after, -2)

    row = after(jnp.arange(BOTH + 16, dtype=jnp.int32), first_step)
    token = jnp.where(row < OWN, row + core * OWN, row - core * OWN)
    token = jnp.where(row < BOTH, token, jnp.where(row < BOTH + 8, row - BOTH - 8, row - 8))
    doc = jnp.where(token < OWN, first_doc, second_doc)
    doc = jnp.where(token < 0, doc_before, jnp.where(token < BOTH, doc, doc_after))
    gap = token[:, None] - token[None, :]
    same = doc[:, None] == doc[None, :]
    shifts = jnp.concatenate([(gap == k) & same for k in (1, 2)], 0).astype(BF)

    edge = jnp.concatenate(
        [
            jnp.where(core == 1, tokens[-8:], tokens[:8]),
            jnp.where(core == 1, cotangent[-8:], cotangent[:8]),
        ],
        0,
    )
    swaps = [(2 * g + 1, 2 * g + 2) for g in range(31)]
    edge = lax.ppermute(after(edge, first_got), SEQ, swaps + [(b, a) for a, b in swaps])
    got = shift(after(jnp.concatenate([tokens, cotangent], 0), first_got), "core", 1)
    edges = by_core(core, edge, shift(edge, "core", 1))
    tokens_all = jnp.concatenate([tokens, got[:OWN], edges[0][:8], edges[1][:8]], 0)
    cot_all = jnp.concatenate([cotangent, got[OWN:], edges[0][8:], edges[1][8:]], 0)
    tokens_all = dot(tokens_all, perm, ((1,), (0,))).astype(BF)
    cot_all = dot(cot_all, perm, ((1,), (0,))).astype(BF)
    cot_pair = dot(cot_all, perm_pair, ((1,), (0,))).astype(BF)
    gains = jnp.dot(norm_gains, perm.astype(F32), precision=exact)
    gain_one, gain_two = gains[0], gains[1]
    taps = jnp.where(core == 0, conv_taps[:, :chans], conv_taps[:, chans:])

    def own_rows(values):
        return jnp.concatenate([values[:OWN], values[BOTH:]], 0)

    def columns(values, i):
        return values[:BOTH, 256 * i : 256 * (i + 1)]

    xf_all = tokens_all.astype(F32)
    scale_all = row_scale(xf_all)
    normed = lax.optimization_barrier((xf_all * scale_all * gain_one).astype(BF))
    xf, scale_one = own_rows(xf_all), scale_all[:OWN]

    w_in, w_out = w_mixer[:, : 3 * chans], w_mixer[:, 3 * chans :]
    proj = dot(normed, w_in, ((1,), (0,)))
    part_b, part_c, part_x = proj[:, :chans], proj[:, chans : 2 * chans], proj[:, 2 * chans :]
    gated_in = (part_b * part_x).astype(BF)
    back = dot(shifts, gated_in, ((1,), (0,)))
    back_one, back_two = back[: BOTH + 16], back[BOTH + 16 :]
    mixed = taps[2] * gated_in.astype(F32) + taps[1] * back_one + taps[0] * back_two
    gated_out = (part_c * mixed).astype(BF)
    mixer_sum = core_sum(dot(gated_out, w_out, ((1,), (1,))))
    resid = xf + pair_sum(mixer_sum)
    scale_two = row_scale(resid)
    normed_two = (resid * scale_two * gain_two).astype(BF)
    normed_two = dot(after(normed_two, cot_pair), perm_pair, ((1,), (0,))).astype(BF)
    normed_two = both_blocks(normed_two)

    grad_feed, dnormed_two, block_part = feed_forward(normed_two, cot_pair, w_feed)
    grad_feed = lax.psum_scatter(grad_feed, ("z", "x"), scatter_dimension=0, tiled=True)
    dnormed_two = core_sum(dnormed_two)
    block_sum = core_sum(block_part)
    dnormed_two = pair_sum(dot(dnormed_two, perm_pair, ((1,), (1,))).astype(BF))
    block_sum = after(dot(block_sum, perm_pair, ((1,), (1,))), dnormed_two).astype(BF)

    cot_own = own_rows(cot_all).astype(F32)
    q_two = dnormed_two * gain_two
    dresid = (
        cot_own
        + scale_two * q_two
        - resid * scale_two**3 * jnp.mean(q_two * resid, axis=1, keepdims=True)
    )
    dgain_two = jnp.sum((dnormed_two * resid * scale_two)[:OWN], axis=0)

    dattn_own = dresid.astype(BF)
    block_sum = pair_sum(block_sum)
    dattn = both_blocks(dattn_own)
    dgated_out = dot(dattn, w_out, ((1,), (0,)))
    dpart_c = (dgated_out * mixed)[:BOTH]
    dmixed = dgated_out * part_c
    tapped = jnp.concatenate([taps[1] * dmixed, taps[0] * dmixed], 0)
    high, lower = halved(tapped)
    ahead = dot(shifts, high, ((0,), (0,))) + dot(shifts, lower, ((0,), (0,)))
    dmixed = dmixed[:BOTH]
    dgated_in = taps[2] * dmixed + ahead[:BOTH]
    dtaps = jnp.stack(
        [
            jnp.sum(dmixed * back_two[:BOTH], axis=0),
            jnp.sum(dmixed * back_one[:BOTH], axis=0),
            jnp.sum(dmixed * gated_in[:BOTH].astype(F32), axis=0),
        ],
        0,
    )
    dproj = jnp.concatenate(
        [dgated_in * part_x[:BOTH], dpart_c, dgated_in * part_b[:BOTH]], 1
    ).astype(BF)
    dproj = lax.optimization_barrier(dproj)

    dnormed_part = dot(dproj, w_in, ((1,), (1,)))
    dgain_one = jnp.sum(dnormed_part * tokens_all[:BOTH].astype(F32) * scale_all[:BOTH], axis=0)
    dgains = jnp.stack([dgain_one, jnp.where(tp == 0, dgain_two, 0.0)], 0)
    dgains = dot(jnp.concatenate(halved(dgains), 0), perm, ((1,), (1,)))
    dgains = dgains[:2] + dgains[2:]
    place = jnp.arange(4, dtype=jnp.int32)[None, :, None] == tp * 2 + core
    dtaps_wide = jnp.where(place, dtaps[:, None, :], 0.0).reshape(3, width)
    small = jnp.concatenate([dgains, dtaps_wide, jnp.zeros((11, width), F32)], 0).astype(BF)
    mixer_pieces = [
        jnp.concatenate(
            [
                jnp.concatenate(
                    [
                        dot(columns(normed, i), dproj, ((0,), (0,))).astype(BF),
                        dot(columns(dattn, i), gated_out[:BOTH], ((0,), (0,))).astype(BF),
                    ],
                    1,
                ),
                small,
            ],
            0,
        )
        for i in range(4)
    ]
    dnormed = core_sum(dnormed_part)
    ready = block_sum[:1] + dnormed[:1].astype(F32)
    grad_mixer = scatter_ring(mixer_pieces, "z", ready)
    dnormed = pair_sum(dnormed)
    grad_mixer = scatter_second(after(grad_mixer, dnormed))
    block_rel = (resid[:OWN] + block_sum).astype(BF)
    block_out = dot(block_rel, perm, ((1,), (1,))).astype(BF)

    q_one = dnormed * gain_one
    xf = xf[:OWN]
    grad_rel = (
        dresid[:OWN]
        + scale_one * q_one
        - xf * scale_one**3 * jnp.mean(q_one * xf, axis=1, keepdims=True)
    )
    high, lower = halved(grad_rel)
    grad_tokens = dot(high, perm, ((1,), (1,))) + dot(lower, perm, ((1,), (1,)))

    grads = jnp.concatenate([grad_feed, after(after(grad_mixer[:64], grad_tokens), block_out).astype(BF)], 1)
    small = jnp.pad(grad_mixer[64:69].reshape(1, -1), ((0, 0), (0, 2 * grads.shape[1] - 5 * width)))
    grads, small = scatter_pair(grads, small.reshape(2, grads.shape[1]), core)
    small = small.reshape(-1)[: 5 * width].reshape(5, width)
    small = small + shift(small, "tp", 1)
    grad_gains = small[:2]
    half = width // 2
    grad_taps = jnp.where(tp == 0, small[2:, :half], small[2:, half:])


    def joined(parts, shape):
        parts = [p.reshape(shape[:-1] + (1, shape[-1])) for p in parts]
        return jnp.concatenate(parts, len(shape) - 1).reshape(shape[:-1] + (2 * shape[-1],))

    ends = (3 * hidden, 3 * hidden + 3 * chans)
    grad_up = joined([g[:, : 2 * hidden] for g in grads], (16, 2, hidden))
    grad_down = joined([g[:, 2 * hidden : 3 * hidden] for g in grads], (16, hidden))
    grad_in = joined([g[:, ends[0] : ends[1]] for g in grads], (16, 3, chans))
    grad_out = joined([g[:, ends[1] :] for g in grads], (16, chans))
    return (
        block_out,
        grad_tokens,
        *adamw(inward_weight, grad_in, inward_first, inward_second, 0.05, 0.1),
        *adamw(outward_weight, grad_out, outward_first, outward_second, 0.05, 0.1),
        *adamw(expand_weight, grad_up, expand_first, expand_second, 0.05, 0.1),
        *adamw(reduce_weight, grad_down, reduce_first, reduce_second, 0.05, 0.1),
        *adamw(norm_gains, grad_gains, gains_first, gains_second, 0.5, 0.0),
        *adamw(conv_taps, grad_taps, taps_first, taps_second, 0.5, 0.0),
    )


def solution(mesh):
    fine = Mesh(mesh.devices.reshape(4, 2, 4, 2, 2), ("z", "yh", "x", "core", "tp"))
    rows = P(SEQ, None)
    wide, flat, tap = P(SEQ, None, "tp"), P(SEQ, "tp"), P(None, "tp")
    weights = (wide,) * 3 + (flat,) * 3 + (wide,) * 3 + (flat,) * 3
    small = (P(),) * 3 + (tap,) * 3
    return jax.shard_map(
        body,
        mesh=fine,
        in_specs=(rows, rows, P()) + weights + small,
        out_specs=(rows, rows) + weights + small,
        check_vma=False,
    )
```

```python
import jax
import jax.numpy as jnp
from jax import lax
from jax.experimental import pallas as pl
from jax.experimental.pallas import tpu as pltpu
from jax.sharding import Mesh
from jax.sharding import PartitionSpec as P

STEP = 8
BF = jnp.bfloat16
F32 = jnp.float32
SEQ = ("z", "yh", "x", "core")


def shift(value, axis, steps):
    count = lax.axis_size(axis)
    return lax.ppermute(value, axis, [(i, (i + steps) % count) for i in range(count)])


def dot(a, b, dims):
    return lax.dot_general(a, b, (dims, ((), ())), preferred_element_type=F32)


def row_scale(values):
    return lax.rsqrt(jnp.mean(values * values, axis=1, keepdims=True) + 1e-05)


def adamw(weight, grad, first, second, rate, decay):
    first_new = 0.9 * first + 0.1 * grad
    second_new = 0.95 * second + 0.05 * grad * grad
    step_size = first_new / (1.0 - 0.9**STEP) / (jnp.sqrt(second_new / (1.0 - 0.95**STEP)) + 1e-08)
    return (weight - rate * (step_size + decay * weight), first_new, second_new)


def gather_direct(block, axis):
    return [block, shift(block, axis, -1), shift(block, axis, 2), shift(block, axis, 1)]


def gather_ring(block, axis):
    half = block.shape[0] // 2
    left = shift(block, axis, 1)
    right = shift(block, axis, -1)
    low = shift(right[:half], axis, -1)
    high = shift(left[half:], axis, 1)
    return [block, right, jnp.concatenate([low, high], 0), left]


def add(*terms):
    total = terms[0].astype(F32)
    for term in terms[1:]:
        total = total + term.astype(F32)
    return total


def scatter_direct(pieces, axis):
    one = shift(pieces[1], axis, 1)
    three = shift(pieces[3], axis, -1)
    two = shift(pieces[2], axis, 2)
    return add(pieces[0], one, two, three)


def scatter_ring(pieces, axis, before):
    own, one, two, three = pieces
    half = two.shape[0] // 32 * 16
    low = shift(two[:half], axis, 1)
    high = shift(two[half:], axis, -1)
    one = jnp.concatenate([after(add(one[:half], low), before).astype(BF), one[half:]], 0)
    three = jnp.concatenate([three[:half], after(add(three[half:], high), before).astype(BF)], 0)
    return add(own, shift(one, axis, 1), shift(three, axis, -1))


def gather_rows(rows):
    cols = rows.shape[1]
    along_x = gather_direct(rows, "x")
    part = jnp.stack([p.reshape(2, 32, cols) for p in along_x], 1)
    pieces = gather_ring(part.reshape(256, cols), "z")
    return jnp.concatenate(pieces, 0), along_x[3], pieces[1]


def scatter_second(part):
    cols = part.shape[1]
    part = part.astype(BF)
    blocks = part[:256].reshape(2, 4, 32, cols)
    pieces = [jnp.concatenate([blocks[:, i].reshape(64, cols), part[256:]], 0) for i in range(4)]
    return scatter_direct(pieces, "x")


def swap_diagonal(value):
    return lax.ppermute(value, ("yh", "core"), [(i, 3 - i) for i in range(4)])


def halved(value):
    high = value.astype(BF)
    return high, (value - high.astype(F32)).astype(BF)


def by_core(core, own, other):
    return jnp.where(core == 0, own, other), jnp.where(core == 0, other, own)


def gather_pair(mine, theirs, core):
    here = by_core(core, mine, shift(theirs, "core", 1))
    there = by_core(core, shift(mine, "yh", 1), swap_diagonal(theirs))
    return jnp.concatenate(here + there, 0)


def scatter_pair(part, small, core):
    part, small = part.astype(BF), small.astype(BF)
    here, there = part[:32], part[32:]

    def pick(rows, own):
        first, second = (rows[:16], rows[16:]) if own else (rows[16:], rows[:16])
        return jnp.concatenate([jnp.where(core == 0, first, second), small], 0)

    got = shift(pick(there, True), "yh", 1)
    got_core = shift(pick(here, False), "core", 1)
    got_diagonal = swap_diagonal(pick(there, False))
    own = add(pick(here, True), got)
    other = add(got_core, got_diagonal)
    return by_core(core, own[:16], other[:16]), own[16:] + other[16:]


OWN, BOTH = 256, 512


def core_sum(partial):
    partial = partial.astype(BF)
    extra = partial[BOTH:]
    got = shift(jnp.concatenate([partial[OWN:BOTH], extra], 0), "core", 1)
    return add(jnp.concatenate([partial[:OWN], extra], 0), got).astype(BF)


def pair_sum(own):
    return add(own, shift(own, "tp", 1))


def both_blocks(own):
    return jnp.concatenate([own[:OWN], shift(own[:OWN], "core", 1), own[OWN:]], 0)


def feed_forward_kernel(
    normed_ref, cot_ref, weights_ref, grads_ref, dnormed_ref, block_ref, held, sums, came, left
):
    cols = held.shape[2]
    span = [pl.ds(k * cols, cols) for k in range(3)]
    arriving = [
        pltpu.make_async_copy(weights_ref.at[:, span[k]], held.at[k], came.at[k]) for k in range(3)
    ]
    leaving = [
        pltpu.make_async_copy(sums.at[k], grads_ref.at[:, span[k]], left.at[k]) for k in range(3)
    ]
    for k in (2, 0, 1):
        arriving[k].start()
    arriving[2].wait()
    dact = dot(cot_ref[...], held[2], ((1,), (0,)))
    arriving[0].wait()
    gate = dot(normed_ref[...], held[0], ((1,), (0,)))
    arriving[1].wait()
    upper = dot(normed_ref[...], held[1], ((1,), (0,)))
    sigma = jax.nn.sigmoid(gate)
    silu = gate * sigma
    act = (silu * upper).astype(BF)
    dgate = (dact * upper * sigma * (1.0 + gate * (1.0 - sigma))).astype(BF)
    dupper = (dact * silu).astype(BF)
    normed, cot = normed_ref[:BOTH], cot_ref[:BOTH]
    for k, rows, grad in ((0, normed, dgate), (1, normed, dupper), (2, cot, act)):
        sums[k] = dot(rows, grad[:BOTH], ((0,), (0,))).astype(BF)
        leaving[k].start()
    dnormed = dot(dgate, held[0], ((1,), (1,))) + dot(dupper, held[1], ((1,), (1,)))
    dnormed_ref[...] = dnormed.astype(BF)
    block_ref[...] = dot(act[:BOTH], held[2], ((1,), (1,))).astype(BF)
    for copy in leaving:
        copy.wait()


def feed_forward(normed, cot, weights):
    rows, width = normed.shape
    cols = weights.shape[1] // 3
    vmem, hbm = pl.BlockSpec(memory_space=pltpu.VMEM), pl.BlockSpec(memory_space=pl.ANY)
    return pl.pallas_call(
        feed_forward_kernel,
        in_specs=[vmem, vmem, hbm],
        out_specs=[hbm, vmem, vmem],
        out_shape=[
            jax.ShapeDtypeStruct(weights.shape, BF),
            jax.ShapeDtypeStruct((rows, width), BF),
            jax.ShapeDtypeStruct((BOTH, width), BF),
        ],
        scratch_shapes=[
            pltpu.VMEM((3, width, cols), BF),
            pltpu.VMEM((3, width, cols), BF),
            pltpu.SemaphoreType.DMA((3,)),
            pltpu.SemaphoreType.DMA((3,)),
        ],
        compiler_params=pltpu.CompilerParams(vmem_limit_bytes=48 * 2**20),
        cost_estimate=pl.CostEstimate(
            flops=18 * rows * width * cols,
            bytes_accessed=4 * weights.size,
            transcendentals=rows * cols,
        ),
    )(normed, cot, weights)


def after(value, before):
    if before is None:
        return value
    corner = before[tuple(slice(0, 1) for _ in before.shape)].reshape((1,) * value.ndim)
    if value.dtype == jnp.int32:
        return value + (corner.astype(F32) > 3e38).astype(jnp.int32)
    return value + corner.astype(value.dtype) * 0


def body(
    tokens,
    cotangent,
    doc_ids,
    inward_weight,
    inward_first,
    inward_second,
    outward_weight,
    outward_first,
    outward_second,
    expand_weight,
    expand_first,
    expand_second,
    reduce_weight,
    reduce_first,
    reduce_second,
    norm_gains,
    gains_first,
    gains_second,
    conv_taps,
    taps_first,
    taps_second,
):
    z, yh, x = lax.axis_index("z"), lax.axis_index("yh"), lax.axis_index("x")
    core, tp = lax.axis_index("core"), lax.axis_index("tp")
    width = tokens.shape[1]
    chans = inward_weight.shape[2] // 2
    hidden = expand_weight.shape[2] // 2

    def split(weight):
        halves = weight.astype(BF).reshape(weight.shape[:-1] + (2, weight.shape[-1] // 2))
        pair = by_core(core, halves[..., 0, :], halves[..., 1, :])
        return [p.reshape(16, -1) for p in pair]

    quarters = zip(*[split(w) for w in (expand_weight, reduce_weight, inward_weight, outward_weight)])
    all_pair = gather_pair(*[jnp.concatenate(q, 1) for q in quarters], core)
    feed_pair, mixer_pair = all_pair[:, : 3 * hidden], all_pair[:, 3 * hidden :]
    w_feed = lax.all_gather(feed_pair, ("z", "x"), axis=0, tiled=True)
    w_mixer, first_x, first_step = gather_rows(mixer_pair)

    index = after(jnp.arange(width, dtype=jnp.int32), first_step)
    low = index % 32
    rel_z, rel_y, rel_x = (z + index // 256) % 4, (yh + index // 128) % 2, (x + index // 32) % 4
    relative = ((rel_z * 2 + rel_y) * 4 + rel_x) * 32 + low
    pair = ((index // 256 * 2 + (yh + index // 32) % 2) * 4 + index // 64 % 4) * 32 + low
    perm = (index[:, None] == relative[None, :]).astype(BF)
    perm_pair = (relative[:, None] == pair[None, :]).astype(BF)
    exact = lax.Precision.HIGHEST

    gidx = (z * 2 + yh) * 4 + x
    first_doc, second_doc = doc_ids[2 * gidx], doc_ids[2 * gidx + 1]
    doc_before = doc_ids[jnp.maximum(2 * gidx - 1, 0)]
    doc_after = doc_ids[jnp.minimum(2 * gidx + 2, 63)]
    doc_before = jnp.where(gidx > 0, doc_before, -1)
    doc_after = jnp.where(gidx < 31, doc_after, -2)

    row = after(jnp.arange(BOTH + 16, dtype=jnp.int32), first_step)
    token = jnp.where(row < OWN, row + core * OWN, row - core * OWN)
    token = jnp.where(row < BOTH, token, jnp.where(row < BOTH + 8, row - BOTH - 8, row - 8))
    doc = jnp.where(token < OWN, first_doc, second_doc)
    doc = jnp.where(token < 0, doc_before, jnp.where(token < BOTH, doc, doc_after))
    gap = token[:, None] - token[None, :]
    same = doc[:, None] == doc[None, :]
    shifts = jnp.concatenate([(gap == k) & same for k in (1, 2)], 0).astype(BF)

    edge = jnp.concatenate(
        [
            jnp.where(core == 1, tokens[-8:], tokens[:8]),
            jnp.where(core == 1, cotangent[-8:], cotangent[:8]),
        ],
        0,
    )
    swaps = [(2 * g + 1, 2 * g + 2) for g in range(31)]
    edge = lax.ppermute(after(edge, first_x), SEQ, swaps + [(b, a) for a, b in swaps])
    got = shift(after(jnp.concatenate([tokens, cotangent], 0), first_x), "core", 1)
    edges = by_core(core, edge, shift(edge, "core", 1))
    tokens_all = jnp.concatenate([tokens, got[:OWN], edges[0][:8], edges[1][:8]], 0)
    cot_all = jnp.concatenate([cotangent, got[OWN:], edges[0][8:], edges[1][8:]], 0)
    tokens_all = dot(tokens_all, perm, ((1,), (0,))).astype(BF)
    cot_all = dot(cot_all, perm, ((1,), (0,))).astype(BF)
    cot_pair = dot(cot_all, perm_pair, ((1,), (0,))).astype(BF)
    gains = jnp.dot(norm_gains, perm.astype(F32), precision=exact)
    gain_one, gain_two = gains[0], gains[1]
    taps = jnp.where(core == 0, conv_taps[:, :chans], conv_taps[:, chans:])

    def own_rows(values):
        return jnp.concatenate([values[:OWN], values[BOTH:]], 0)

    def columns(values, i):
        return values[:BOTH, 256 * i : 256 * (i + 1)]

    xf_all = tokens_all.astype(F32)
    scale_all = row_scale(xf_all)
    normed = lax.optimization_barrier((xf_all * scale_all * gain_one).astype(BF))
    xf, scale_one = own_rows(xf_all), scale_all[:OWN]

    w_in, w_out = w_mixer[:, : 3 * chans], w_mixer[:, 3 * chans :]
    proj = dot(normed, w_in, ((1,), (0,)))
    part_b, part_c, part_x = proj[:, :chans], proj[:, chans : 2 * chans], proj[:, 2 * chans :]
    gated_in = (part_b * part_x).astype(BF)
    back = dot(shifts, gated_in, ((1,), (0,)))
    back_one, back_two = back[: BOTH + 16], back[BOTH + 16 :]
    mixed = taps[2] * gated_in.astype(F32) + taps[1] * back_one + taps[0] * back_two
    gated_out = (part_c * mixed).astype(BF)
    mixer_sum = core_sum(dot(gated_out, w_out, ((1,), (1,))))
    resid = xf + pair_sum(mixer_sum)
    scale_two = row_scale(resid)
    normed_two = (resid * scale_two * gain_two).astype(BF)
    normed_two = dot(after(normed_two, cot_pair), perm_pair, ((1,), (0,))).astype(BF)
    normed_two = both_blocks(normed_two)

    grad_feed, dnormed_two, block_part = feed_forward(normed_two, cot_pair, w_feed)
    grad_feed = lax.psum_scatter(grad_feed, ("z", "x"), scatter_dimension=0, tiled=True)
    dnormed_two = core_sum(dnormed_two)
    block_sum = core_sum(block_part)
    dnormed_two = pair_sum(dot(dnormed_two, perm_pair, ((1,), (1,))).astype(BF))
    block_sum = after(dot(block_sum, perm_pair, ((1,), (1,))), dnormed_two).astype(BF)

    cot_own = own_rows(cot_all).astype(F32)
    q_two = dnormed_two * gain_two
    dresid = (
        cot_own
        + scale_two * q_two
        - resid * scale_two**3 * jnp.mean(q_two * resid, axis=1, keepdims=True)
    )
    dgain_two = jnp.sum((dnormed_two * resid * scale_two)[:OWN], axis=0)

    dattn_own = dresid.astype(BF)
    dattn = both_blocks(dattn_own)
    dgated_out = dot(dattn, w_out, ((1,), (0,)))
    dpart_c = (dgated_out * mixed)[:BOTH]
    dmixed = dgated_out * part_c
    tapped = jnp.concatenate([taps[1] * dmixed, taps[0] * dmixed], 0)
    high, lower = halved(tapped)
    ahead = dot(shifts, high, ((0,), (0,))) + dot(shifts, lower, ((0,), (0,)))
    dmixed = dmixed[:BOTH]
    dgated_in = taps[2] * dmixed + ahead[:BOTH]
    dtaps = jnp.stack(
        [
            jnp.sum(dmixed * back_two[:BOTH], axis=0),
            jnp.sum(dmixed * back_one[:BOTH], axis=0),
            jnp.sum(dmixed * gated_in[:BOTH].astype(F32), axis=0),
        ],
        0,
    )
    dproj = jnp.concatenate(
        [dgated_in * part_x[:BOTH], dpart_c, dgated_in * part_b[:BOTH]], 1
    ).astype(BF)
    dproj = lax.optimization_barrier(dproj)

    dnormed_part = dot(dproj, w_in, ((1,), (1,)))
    dgain_one = jnp.sum(dnormed_part * tokens_all[:BOTH].astype(F32) * scale_all[:BOTH], axis=0)
    dgains = jnp.stack([dgain_one, jnp.where(tp == 0, dgain_two, 0.0)], 0)
    dgains = dot(jnp.concatenate(halved(dgains), 0), perm, ((1,), (1,)))
    dgains = dgains[:2] + dgains[2:]
    place = jnp.arange(4, dtype=jnp.int32)[None, :, None] == tp * 2 + core
    dtaps_wide = jnp.where(place, dtaps[:, None, :], 0.0).reshape(3, width)
    small = jnp.concatenate([dgains, dtaps_wide, jnp.zeros((11, width), F32)], 0).astype(BF)
    mixer_pieces = [
        jnp.concatenate(
            [
                jnp.concatenate(
                    [
                        dot(columns(normed, i), dproj, ((0,), (0,))).astype(BF),
                        dot(columns(dattn, i), gated_out[:BOTH], ((0,), (0,))).astype(BF),
                    ],
                    1,
                ),
                small,
            ],
            0,
        )
        for i in range(4)
    ]
    block_sum = add(after(block_sum, dnormed_part), shift(block_sum, "tp", 1))
    dnormed = core_sum(dnormed_part)
    ready = block_sum[:1] + dnormed[:1].astype(F32)
    grad_mixer = scatter_ring(mixer_pieces, "z", ready)
    dnormed = pair_sum(dnormed)
    grad_mixer = scatter_second(after(grad_mixer, dnormed))
    block_rel = (resid[:OWN] + block_sum).astype(BF)
    block_out = dot(block_rel, perm, ((1,), (1,))).astype(BF)

    q_one = dnormed * gain_one
    xf = xf[:OWN]
    grad_rel = (
        dresid[:OWN]
        + scale_one * q_one
        - xf * scale_one**3 * jnp.mean(q_one * xf, axis=1, keepdims=True)
    )
    high, lower = halved(grad_rel)
    grad_tokens = dot(high, perm, ((1,), (1,))) + dot(lower, perm, ((1,), (1,)))

    grads = jnp.concatenate([grad_feed, after(after(grad_mixer[:64], grad_tokens), block_out).astype(BF)], 1)
    small = jnp.pad(grad_mixer[64:69].reshape(1, -1), ((0, 0), (0, 2 * grads.shape[1] - 5 * width)))
    grads, small = scatter_pair(grads, small.reshape(2, grads.shape[1]), core)
    small = small.reshape(-1)[: 5 * width].reshape(5, width)
    small = small + shift(small, "tp", 1)
    grad_gains = small[:2]
    half = width // 2
    grad_taps = jnp.where(tp == 0, small[2:, :half], small[2:, half:])


    def joined(parts, shape):
        parts = [p.reshape(shape[:-1] + (1, shape[-1])) for p in parts]
        return jnp.concatenate(parts, len(shape) - 1).reshape(shape[:-1] + (2 * shape[-1],))

    ends = (3 * hidden, 3 * hidden + 3 * chans)
    grad_up = joined([g[:, : 2 * hidden] for g in grads], (16, 2, hidden))
    grad_down = joined([g[:, 2 * hidden : 3 * hidden] for g in grads], (16, hidden))
    grad_in = joined([g[:, ends[0] : ends[1]] for g in grads], (16, 3, chans))
    grad_out = joined([g[:, ends[1] :] for g in grads], (16, chans))
    return (
        block_out,
        grad_tokens,
        *adamw(inward_weight, grad_in, inward_first, inward_second, 0.05, 0.1),
        *adamw(outward_weight, grad_out, outward_first, outward_second, 0.05, 0.1),
        *adamw(expand_weight, grad_up, expand_first, expand_second, 0.05, 0.1),
        *adamw(reduce_weight, grad_down, reduce_first, reduce_second, 0.05, 0.1),
        *adamw(norm_gains, grad_gains, gains_first, gains_second, 0.5, 0.0),
        *adamw(conv_taps, grad_taps, taps_first, taps_second, 0.5, 0.0),
    )


def solution(mesh):
    fine = Mesh(mesh.devices.reshape(4, 2, 4, 2, 2), ("z", "yh", "x", "core", "tp"))
    rows = P(SEQ, None)
    wide, flat, tap = P(SEQ, None, "tp"), P(SEQ, "tp"), P(None, "tp")
    weights = (wide,) * 3 + (flat,) * 3 + (wide,) * 3 + (flat,) * 3
    small = (P(),) * 3 + (tap,) * 3
    return jax.shard_map(
        body,
        mesh=fine,
        in_specs=(rows, rows, P()) + weights + small,
        out_specs=(rows, rows) + weights + small,
        check_vma=False,
    )
```

```python
import jax
import jax.numpy as jnp
from jax import lax
from jax.experimental import pallas as pl
from jax.experimental.pallas import tpu as pltpu
from jax.sharding import Mesh
from jax.sharding import PartitionSpec as P

STEP = 8
BF = jnp.bfloat16
F32 = jnp.float32
SEQ = ("z", "yh", "x", "core")


def shift(value, axis, steps):
    count = lax.axis_size(axis)
    return lax.ppermute(value, axis, [(i, (i + steps) % count) for i in range(count)])


def dot(a, b, dims):
    return lax.dot_general(a, b, (dims, ((), ())), preferred_element_type=F32)


def row_scale(values):
    return lax.rsqrt(jnp.mean(values * values, axis=1, keepdims=True) + 1e-05)


def adamw(weight, grad, first, second, rate, decay):
    first_new = 0.9 * first + 0.1 * grad
    second_new = 0.95 * second + 0.05 * grad * grad
    step_size = first_new / (1.0 - 0.9**STEP) / (jnp.sqrt(second_new / (1.0 - 0.95**STEP)) + 1e-08)
    return (weight - rate * (step_size + decay * weight), first_new, second_new)


def gather_direct(block, axis):
    return [block, shift(block, axis, -1), shift(block, axis, 2), shift(block, axis, 1)]


def gather_ring(block, axis):
    half = block.shape[0] // 2
    left = shift(block, axis, 1)
    right = shift(block, axis, -1)
    low = shift(right[:half], axis, -1)
    high = shift(left[half:], axis, 1)
    return [block, right, jnp.concatenate([low, high], 0), left]


def add(*terms):
    total = terms[0].astype(F32)
    for term in terms[1:]:
        total = total + term.astype(F32)
    return total


def scatter_direct(pieces, axis):
    one = shift(pieces[1], axis, 1)
    three = shift(pieces[3], axis, -1)
    two = shift(pieces[2], axis, 2)
    return add(pieces[0], one, two, three)


def scatter_ring(pieces, axis, before):
    own, one, two, three = pieces
    half = two.shape[0] // 32 * 16
    low = shift(two[:half], axis, 1)
    high = shift(two[half:], axis, -1)
    one = jnp.concatenate([after(add(one[:half], low), before).astype(BF), one[half:]], 0)
    three = jnp.concatenate([three[:half], after(add(three[half:], high), before).astype(BF)], 0)
    return add(own, shift(one, axis, 1), shift(three, axis, -1))


def gather_rows(rows):
    cols = rows.shape[1]
    along_x = gather_direct(rows, "x")
    part = jnp.stack([p.reshape(2, 32, cols) for p in along_x], 1)
    pieces = gather_ring(part.reshape(256, cols), "z")
    return jnp.concatenate(pieces, 0), along_x[3], pieces[1]


def scatter_second(part):
    cols = part.shape[1]
    part = part.astype(BF)
    blocks = part[:256].reshape(2, 4, 32, cols)
    pieces = [jnp.concatenate([blocks[:, i].reshape(64, cols), part[256:]], 0) for i in range(4)]
    return scatter_direct(pieces, "x")


def swap_diagonal(value):
    return lax.ppermute(value, ("yh", "core"), [(i, 3 - i) for i in range(4)])


def halved(value):
    high = value.astype(BF)
    return high, (value - high.astype(F32)).astype(BF)


def by_core(core, own, other):
    return jnp.where(core == 0, own, other), jnp.where(core == 0, other, own)


def gather_pair(mine, theirs, core):
    here = by_core(core, mine, shift(theirs, "core", 1))
    there = by_core(core, shift(mine, "yh", 1), swap_diagonal(theirs))
    return jnp.concatenate(here + there, 0)


def scatter_pair(part, small, core):
    part, small = part.astype(BF), small.astype(BF)
    here, there = part[:32], part[32:]

    def pick(rows, own):
        first, second = (rows[:16], rows[16:]) if own else (rows[16:], rows[:16])
        return jnp.concatenate([jnp.where(core == 0, first, second), small], 0)

    got = shift(pick(there, True), "yh", 1)
    got_core = shift(pick(here, False), "core", 1)
    got_diagonal = swap_diagonal(pick(there, False))
    own = add(pick(here, True), got)
    other = add(got_core, got_diagonal)
    return by_core(core, own[:16], other[:16]), own[16:] + other[16:]


OWN, BOTH = 256, 512


def core_sum(partial):
    partial = partial.astype(BF)
    extra = partial[BOTH:]
    got = shift(jnp.concatenate([partial[OWN:BOTH], extra], 0), "core", 1)
    return add(jnp.concatenate([partial[:OWN], extra], 0), got).astype(BF)


def pair_sum(own):
    return add(own, shift(own, "tp", 1))


def both_blocks(own):
    return jnp.concatenate([own[:OWN], shift(own[:OWN], "core", 1), own[OWN:]], 0)


def feed_forward_kernel(
    normed_ref, cot_ref, weights_ref, grads_ref, dnormed_ref, block_ref, held, sums, came, left
):
    cols = held.shape[2]
    span = [pl.ds(k * cols, cols) for k in range(3)]
    arriving = [
        pltpu.make_async_copy(weights_ref.at[:, span[k]], held.at[k], came.at[k]) for k in range(3)
    ]
    leaving = [
        pltpu.make_async_copy(sums.at[k], grads_ref.at[:, span[k]], left.at[k]) for k in range(3)
    ]
    for k in (2, 0, 1):
        arriving[k].start()
    arriving[2].wait()
    dact = dot(cot_ref[...], held[2], ((1,), (0,)))
    arriving[0].wait()
    gate = dot(normed_ref[...], held[0], ((1,), (0,)))
    arriving[1].wait()
    upper = dot(normed_ref[...], held[1], ((1,), (0,)))
    sigma = jax.nn.sigmoid(gate)
    silu = gate * sigma
    act = (silu * upper).astype(BF)
    dgate = (dact * upper * sigma * (1.0 + gate * (1.0 - sigma))).astype(BF)
    dupper = (dact * silu).astype(BF)
    normed, cot = normed_ref[:BOTH], cot_ref[:BOTH]
    for k, rows, grad in ((0, normed, dgate), (1, normed, dupper), (2, cot, act)):
        sums[k] = dot(rows, grad[:BOTH], ((0,), (0,))).astype(BF)
        leaving[k].start()
    dnormed = dot(dgate, held[0], ((1,), (1,))) + dot(dupper, held[1], ((1,), (1,)))
    dnormed_ref[...] = dnormed.astype(BF)
    block_ref[...] = dot(act[:BOTH], held[2], ((1,), (1,))).astype(BF)
    for copy in leaving:
        copy.wait()


def feed_forward(normed, cot, weights):
    rows, width = normed.shape
    cols = weights.shape[1] // 3
    vmem, hbm = pl.BlockSpec(memory_space=pltpu.VMEM), pl.BlockSpec(memory_space=pl.ANY)
    return pl.pallas_call(
        feed_forward_kernel,
        in_specs=[vmem, vmem, hbm],
        out_specs=[hbm, vmem, vmem],
        out_shape=[
            jax.ShapeDtypeStruct(weights.shape, BF),
            jax.ShapeDtypeStruct((rows, width), BF),
            jax.ShapeDtypeStruct((BOTH, width), BF),
        ],
        scratch_shapes=[
            pltpu.VMEM((3, width, cols), BF),
            pltpu.VMEM((3, width, cols), BF),
            pltpu.SemaphoreType.DMA((3,)),
            pltpu.SemaphoreType.DMA((3,)),
        ],
        compiler_params=pltpu.CompilerParams(vmem_limit_bytes=48 * 2**20),
        cost_estimate=pl.CostEstimate(
            flops=18 * rows * width * cols,
            bytes_accessed=4 * weights.size,
            transcendentals=rows * cols,
        ),
    )(normed, cot, weights)


def after(value, before):
    if before is None:
        return value
    corner = before[tuple(slice(0, 1) for _ in before.shape)].reshape((1,) * value.ndim)
    if value.dtype == jnp.int32:
        return value + (corner.astype(F32) > 3e38).astype(jnp.int32)
    return value + corner.astype(value.dtype) * 0


def body(
    tokens,
    cotangent,
    doc_ids,
    inward_weight,
    inward_first,
    inward_second,
    outward_weight,
    outward_first,
    outward_second,
    expand_weight,
    expand_first,
    expand_second,
    reduce_weight,
    reduce_first,
    reduce_second,
    norm_gains,
    gains_first,
    gains_second,
    conv_taps,
    taps_first,
    taps_second,
):
    z, yh, x = lax.axis_index("z"), lax.axis_index("yh"), lax.axis_index("x")
    core, tp = lax.axis_index("core"), lax.axis_index("tp")
    width = tokens.shape[1]
    chans = inward_weight.shape[2] // 2
    hidden = expand_weight.shape[2] // 2

    def split(weight):
        halves = weight.astype(BF).reshape(weight.shape[:-1] + (2, weight.shape[-1] // 2))
        pair = by_core(core, halves[..., 0, :], halves[..., 1, :])
        return [p.reshape(16, -1) for p in pair]

    quarters = zip(*[split(w) for w in (expand_weight, reduce_weight, inward_weight, outward_weight)])
    all_pair = gather_pair(*[jnp.concatenate(q, 1) for q in quarters], core)
    feed_pair, mixer_pair = all_pair[:, : 3 * hidden], all_pair[:, 3 * hidden :]
    w_feed = lax.all_gather(feed_pair, ("z", "x"), axis=0, tiled=True)
    w_mixer, first_x, first_step = gather_rows(mixer_pair)

    index = after(jnp.arange(width, dtype=jnp.int32), first_step)
    low = index % 32
    rel_z, rel_y, rel_x = (z + index // 256) % 4, (yh + index // 128) % 2, (x + index // 32) % 4
    relative = ((rel_z * 2 + rel_y) * 4 + rel_x) * 32 + low
    pair = ((index // 256 * 2 + (yh + index // 32) % 2) * 4 + index // 64 % 4) * 32 + low
    perm = (index[:, None] == relative[None, :]).astype(BF)
    perm_pair = (relative[:, None] == pair[None, :]).astype(BF)
    exact = lax.Precision.HIGHEST

    gidx = (z * 2 + yh) * 4 + x
    first_doc, second_doc = doc_ids[2 * gidx], doc_ids[2 * gidx + 1]
    doc_before = doc_ids[jnp.maximum(2 * gidx - 1, 0)]
    doc_after = doc_ids[jnp.minimum(2 * gidx + 2, 63)]
    doc_before = jnp.where(gidx > 0, doc_before, -1)
    doc_after = jnp.where(gidx < 31, doc_after, -2)

    row = after(jnp.arange(BOTH + 16, dtype=jnp.int32), first_step)
    token = jnp.where(row < OWN, row + core * OWN, row - core * OWN)
    token = jnp.where(row < BOTH, token, jnp.where(row < BOTH + 8, row - BOTH - 8, row - 8))
    doc = jnp.where(token < OWN, first_doc, second_doc)
    doc = jnp.where(token < 0, doc_before, jnp.where(token < BOTH, doc, doc_after))
    gap = token[:, None] - token[None, :]
    same = doc[:, None] == doc[None, :]
    shifts = jnp.concatenate([(gap == k) & same for k in (1, 2)], 0).astype(BF)

    edge = jnp.concatenate(
        [
            jnp.where(core == 1, tokens[-8:], tokens[:8]),
            jnp.where(core == 1, cotangent[-8:], cotangent[:8]),
        ],
        0,
    )
    swaps = [(2 * g + 1, 2 * g + 2) for g in range(31)]
    edge = lax.ppermute(after(edge, first_x), SEQ, swaps + [(b, a) for a, b in swaps])
    got = shift(after(jnp.concatenate([tokens, cotangent], 0), first_x), "core", 1)
    edges = by_core(core, edge, shift(edge, "core", 1))
    tokens_all = jnp.concatenate([tokens, got[:OWN], edges[0][:8], edges[1][:8]], 0)
    cot_all = jnp.concatenate([cotangent, got[OWN:], edges[0][8:], edges[1][8:]], 0)
    tokens_all = dot(tokens_all, perm, ((1,), (0,))).astype(BF)
    cot_all = dot(cot_all, perm, ((1,), (0,))).astype(BF)
    cot_pair = dot(cot_all, perm_pair, ((1,), (0,))).astype(BF)
    gains = jnp.dot(norm_gains, perm.astype(F32), precision=exact)
    gain_one, gain_two = gains[0], gains[1]
    taps = jnp.where(core == 0, conv_taps[:, :chans], conv_taps[:, chans:])

    def own_rows(values):
        return jnp.concatenate([values[:OWN], values[BOTH:]], 0)

    def columns(values, i):
        return values[:BOTH, 256 * i : 256 * (i + 1)]

    xf_all = tokens_all.astype(F32)
    scale_all = row_scale(xf_all)
    normed = lax.optimization_barrier((xf_all * scale_all * gain_one).astype(BF))
    xf, scale_one = own_rows(xf_all), scale_all[:OWN]

    w_in, w_out = w_mixer[:, : 3 * chans], w_mixer[:, 3 * chans :]
    proj = dot(normed, w_in, ((1,), (0,)))
    part_b, part_c, part_x = proj[:, :chans], proj[:, chans : 2 * chans], proj[:, 2 * chans :]
    gated_in = (part_b * part_x).astype(BF)
    back = dot(shifts, gated_in, ((1,), (0,)))
    back_one, back_two = back[: BOTH + 16], back[BOTH + 16 :]
    mixed = taps[2] * gated_in.astype(F32) + taps[1] * back_one + taps[0] * back_two
    gated_out = (part_c * mixed).astype(BF)
    mixer_sum = core_sum(dot(gated_out, w_out, ((1,), (1,))))
    resid = xf + pair_sum(mixer_sum)
    scale_two = row_scale(resid)
    normed_two = (resid * scale_two * gain_two).astype(BF)
    normed_two = dot(after(normed_two, cot_pair), perm_pair, ((1,), (0,))).astype(BF)
    normed_two = both_blocks(normed_two)

    grad_feed, dnormed_two, block_part = feed_forward(normed_two, cot_pair, w_feed)
    grad_feed = lax.psum_scatter(grad_feed, ("z", "x"), scatter_dimension=0, tiled=True)
    dnormed_two = core_sum(dnormed_two)
    block_sum = core_sum(block_part)
    dnormed_two = pair_sum(dot(dnormed_two, perm_pair, ((1,), (1,))).astype(BF))
    block_sum = after(dot(block_sum, perm_pair, ((1,), (1,))), dnormed_two).astype(BF)

    cot_own = own_rows(cot_all).astype(F32)
    q_two = dnormed_two * gain_two
    dresid = (
        cot_own
        + scale_two * q_two
        - resid * scale_two**3 * jnp.mean(q_two * resid, axis=1, keepdims=True)
    )
    dgain_two = jnp.sum((dnormed_two * resid * scale_two)[:OWN], axis=0)

    dattn_own = dresid.astype(BF)
    dattn = both_blocks(dattn_own)
    dgated_out = dot(dattn, w_out, ((1,), (0,)))
    dpart_c = (dgated_out * mixed)[:BOTH]
    dmixed = dgated_out * part_c
    tapped = jnp.concatenate([taps[1] * dmixed, taps[0] * dmixed], 0)
    high, lower = halved(tapped)
    ahead = dot(shifts, high, ((0,), (0,))) + dot(shifts, lower, ((0,), (0,)))
    dmixed = dmixed[:BOTH]
    dgated_in = taps[2] * dmixed + ahead[:BOTH]
    dtaps = jnp.stack(
        [
            jnp.sum(dmixed * back_two[:BOTH], axis=0),
            jnp.sum(dmixed * back_one[:BOTH], axis=0),
            jnp.sum(dmixed * gated_in[:BOTH].astype(F32), axis=0),
        ],
        0,
    )
    dproj = jnp.concatenate(
        [dgated_in * part_x[:BOTH], dpart_c, dgated_in * part_b[:BOTH]], 1
    ).astype(BF)
    dproj = lax.optimization_barrier(dproj)

    dnormed_part = dot(dproj, w_in, ((1,), (1,)))
    dgain_one = jnp.sum(dnormed_part * tokens_all[:BOTH].astype(F32) * scale_all[:BOTH], axis=0)
    dgains = jnp.stack([dgain_one, jnp.where(tp == 0, dgain_two, 0.0)], 0)
    dgains = dot(jnp.concatenate(halved(dgains), 0), perm, ((1,), (1,)))
    dgains = dgains[:2] + dgains[2:]
    place = jnp.arange(4, dtype=jnp.int32)[None, :, None] == tp * 2 + core
    dtaps_wide = jnp.where(place, dtaps[:, None, :], 0.0).reshape(3, width)
    small = jnp.concatenate([dgains, dtaps_wide, jnp.zeros((11, width), F32)], 0).astype(BF)
    mixer_pieces = [
        jnp.concatenate(
            [
                jnp.concatenate(
                    [
                        dot(columns(normed, i), dproj, ((0,), (0,))).astype(BF),
                        dot(columns(dattn, i), gated_out[:BOTH], ((0,), (0,))).astype(BF),
                    ],
                    1,
                ),
                small,
            ],
            0,
        )
        for i in range(4)
    ]
    dnormed = core_sum(dnormed_part)
    block_sum = add(after(block_sum, dnormed), shift(block_sum, "tp", 1))
    ready = block_sum[:1] + dnormed[:1].astype(F32)
    grad_mixer = scatter_ring(mixer_pieces, "z", ready)
    dnormed = pair_sum(dnormed)
    grad_mixer = scatter_second(after(grad_mixer, dnormed))
    block_rel = (resid[:OWN] + block_sum).astype(BF)
    block_out = dot(block_rel, perm, ((1,), (1,))).astype(BF)

    q_one = dnormed * gain_one
    xf = xf[:OWN]
    grad_rel = (
        dresid[:OWN]
        + scale_one * q_one
        - xf * scale_one**3 * jnp.mean(q_one * xf, axis=1, keepdims=True)
    )
    high, lower = halved(grad_rel)
    grad_tokens = dot(high, perm, ((1,), (1,))) + dot(lower, perm, ((1,), (1,)))

    grads = jnp.concatenate([grad_feed, after(after(grad_mixer[:64], grad_tokens), block_out).astype(BF)], 1)
    small = jnp.pad(grad_mixer[64:69].reshape(1, -1), ((0, 0), (0, 2 * grads.shape[1] - 5 * width)))
    grads, small = scatter_pair(grads, small.reshape(2, grads.shape[1]), core)
    small = small.reshape(-1)[: 5 * width].reshape(5, width)
    small = small + shift(small, "tp", 1)
    grad_gains = small[:2]
    half = width // 2
    grad_taps = jnp.where(tp == 0, small[2:, :half], small[2:, half:])


    def joined(parts, shape):
        parts = [p.reshape(shape[:-1] + (1, shape[-1])) for p in parts]
        return jnp.concatenate(parts, len(shape) - 1).reshape(shape[:-1] + (2 * shape[-1],))

    ends = (3 * hidden, 3 * hidden + 3 * chans)
    grad_up = joined([g[:, : 2 * hidden] for g in grads], (16, 2, hidden))
    grad_down = joined([g[:, 2 * hidden : 3 * hidden] for g in grads], (16, hidden))
    grad_in = joined([g[:, ends[0] : ends[1]] for g in grads], (16, 3, chans))
    grad_out = joined([g[:, ends[1] :] for g in grads], (16, chans))
    return (
        block_out,
        grad_tokens,
        *adamw(inward_weight, grad_in, inward_first, inward_second, 0.05, 0.1),
        *adamw(outward_weight, grad_out, outward_first, outward_second, 0.05, 0.1),
        *adamw(expand_weight, grad_up, expand_first, expand_second, 0.05, 0.1),
        *adamw(reduce_weight, grad_down, reduce_first, reduce_second, 0.05, 0.1),
        *adamw(norm_gains, grad_gains, gains_first, gains_second, 0.5, 0.0),
        *adamw(conv_taps, grad_taps, taps_first, taps_second, 0.5, 0.0),
    )


def solution(mesh):
    fine = Mesh(mesh.devices.reshape(4, 2, 4, 2, 2), ("z", "yh", "x", "core", "tp"))
    rows = P(SEQ, None)
    wide, flat, tap = P(SEQ, None, "tp"), P(SEQ, "tp"), P(None, "tp")
    weights = (wide,) * 3 + (flat,) * 3 + (wide,) * 3 + (flat,) * 3
    small = (P(),) * 3 + (tap,) * 3
    return jax.shard_map(
        body,
        mesh=fine,
        in_specs=(rows, rows, P()) + weights + small,
        out_specs=(rows, rows) + weights + small,
        check_vma=False,
    )
```
